32 devices in a mesh: section: 4 (over z), seq: 2 (over y), tp: 4 (over x, core).
Axes of the slice: x: 2, y: 2, z: 4, core: 2. Of those that a mesh axis runs over, the one named last changes fastest.
Arguments:
- text_rows: bfloat16 [128, 8192], P(None, ('seq', 'tp')), may hold values from -6 to 6
- image_rows: bfloat16 [128, 8192], P(('seq', 'tp')), may hold values from -6 to 6
- image_target: int32 [128], P(('seq', 'tp')), may hold values from -1 to 63, as said below
- norm_gain: bfloat16 [4, 8192], P('section', ('seq', 'tp')), may hold values from 0.099609375 to 1.8984375
- q_weight: bfloat16 [4, 8192, 1024], P('section', None, ('seq', 'tp')), may hold values from -0.0625 to 0.0625
- q_bias: bfloat16 [4, 1024], P('section', ('seq', 'tp')), may hold values from -3 to 3
- kv_weight: bfloat16 [4, 8192, 4, 256], P('section', None, 'tp'), may hold values from -0.0625 to 0.0625
- kv_bias: bfloat16 [4, 4, 256], P('section', 'tp'), may hold values from -3 to 3
- out_weight: bfloat16 [4, 1024, 8192], P('section', None, ('seq', 'tp')), may hold values from -0.1875 to 0.1875
Outputs:
- layer_outputs: bfloat16 [4, 128, 8192], P('section', None, ('seq', 'tp'))
The draws below stay inside these ranges and needn't reach their ends.
Inputs may be any that keep to these rules, and one draw needn't show every extreme that they name: `image_target`: in each micro-batch's 64 entries exactly 56 are token positions, all different, and the others are -1.
All inputs are finite; a program needn't handle non-finite values.
Results may differ from the reference program's by a relative error of at most 0.015.
Values may be sent and summed in bfloat16 or wider, within the bound.
A program may use at most 64 MiB of HBM per device.

```python
import math
import jax
import jax.numpy as jnp
from jax import lax

D = 8192
HD = 128
SEQ_TOK = 64
MICRO = 2
QH = 8
KVH = 4
LAYERS = 4
SLOTS = 64
IMG = 56


def draw_image_target(key, part):

    def draw_micro(micro_key):
        key_order, key_place = jax.random.split(micro_key, 2)
        ranks = jax.random.permutation(key_order, SLOTS).astype(jnp.int32)
        rest = jax.random.permutation(key_place, SEQ_TOK - 1).astype(jnp.int32)
        places = jnp.concatenate([jnp.full((1,), SEQ_TOK - 1, jnp.int32), rest]).astype(jnp.int32)
        chosen = places[jnp.minimum(ranks, SEQ_TOK - 1)]
        return jnp.where(ranks < IMG, chosen, -1).astype(jnp.int32)
    micro_keys = jax.random.split(key, MICRO)
    return jax.vmap(draw_micro)(micro_keys).reshape(MICRO * SLOTS).astype(jnp.int32)


def level_of(own_key, dims, cuts, low, top_value):
    factor_of, own = 1.0, jax.random.fold_in(own_key, 6)
    for axis_at, parts in cuts:
        steps = jnp.exp(jax.random.uniform(jax.random.fold_in(own, axis_at), (parts,), jnp.float32, low / len(cuts), top_value / len(cuts)))
        factor_of = factor_of * jnp.repeat(steps, dims[axis_at] // parts).reshape([-1 if axis == axis_at else 1 for axis in range(len(dims))])
    return factor_of


def noise(stream_key, extent, deviation, reach, pieces=(), kind=jnp.bfloat16):
    values = deviation * jax.random.normal(stream_key, extent, jnp.float32)
    if pieces:
        values = values * level_of(stream_key, extent, pieces, -0.22, 0.18)
    return jnp.clip(values, -reach, reach).astype(kind)


def setup_inputs(seed: int = 0) -> dict:
    arg_keys = jax.random.split(jax.random.key(seed), 10)
    return {
        "text_rows": noise(arg_keys[0], (MICRO * SEQ_TOK, D), 1.0, 6.0, ((1, 8),)),
        "image_rows": noise(arg_keys[1], (MICRO * SLOTS, D), 1.0, 6.0, ((0, 8),)),
        "image_target": draw_image_target(jax.random.fold_in(arg_keys[9], 71), 0),
        "norm_gain": jnp.clip(1.0 + 0.18 * jax.random.normal(arg_keys[3], (LAYERS, D), jnp.float32), 0.099609375, 1.8984375).astype(jnp.bfloat16),
        "q_weight": noise(arg_keys[4], (LAYERS, D, QH * HD), D ** -0.5, 0.0625, ((0, 4), (2, 8))),
        "q_bias": noise(arg_keys[5], (LAYERS, QH * HD), 0.5, 3.0, ((0, 4), (1, 8))),
        "kv_weight": noise(arg_keys[6], (LAYERS, D, KVH, 2 * HD), D ** -0.5, 0.0625, ((0, 4), (2, 4))),
        "kv_bias": noise(arg_keys[7], (LAYERS, KVH, 2 * HD), 0.5, 3.0, ((0, 4), (1, 4))),
        "out_weight": noise(arg_keys[8], (LAYERS, QH * HD, D), (QH * HD) ** -0.5, 0.1875, ((0, 4), (2, 8))),
    }


EPS = 1e-06
THETA = 1000000.0

def rotate(values, cosine, sine_tab):
    half_size = values.shape[-1] // 2
    turned = jnp.concatenate([-values[..., half_size:], values[..., :half_size]], axis=-1)
    return values * cosine + turned * sine_tab

def reference(text_rows, image_rows, image_target, norm_gain, q_weight, q_bias, kv_weight, kv_bias, out_weight):
    slot_grid = image_target.reshape(MICRO, SLOTS)
    positions = jnp.arange(SEQ_TOK, dtype=jnp.int32)
    matched = slot_grid[:, None, :] == positions[None, :, None]
    pictures = image_rows.reshape(MICRO, SLOTS, D).astype(jnp.float32)
    placed = jnp.einsum('mps,msd->mpd', matched.astype(jnp.float32), pictures, precision=lax.Precision.HIGHEST)
    is_image = jnp.any(matched, axis=-1)
    text_grid = text_rows.reshape(MICRO, SEQ_TOK, D).astype(jnp.float32)
    hidden = jnp.where(is_image[..., None], placed, text_grid).astype(jnp.bfloat16)
    half_size = HD // 2
    frequency = THETA ** (-jnp.arange(half_size, dtype=jnp.float32) * 2.0 / HD)
    angles = positions.astype(jnp.float32)[:, None] * frequency[None, :]
    cosine = jnp.concatenate([jnp.cos(angles), jnp.cos(angles)], axis=-1)[:, None, :]
    sine_tab = jnp.concatenate([jnp.sin(angles), jnp.sin(angles)], axis=-1)[:, None, :]
    causal = positions[:, None] >= positions[None, :]
    head_group = jnp.arange(QH) % KVH
    collected = []
    for layer in range(LAYERS):
        residual = hidden.reshape(MICRO * SEQ_TOK, D).astype(jnp.float32)
        inv_rms = lax.rsqrt(lax.optimization_barrier(jnp.mean(residual * residual, axis=-1, keepdims=True)) + EPS)
        normed = (residual * inv_rms * norm_gain[layer].astype(jnp.float32)).astype(jnp.bfloat16)
        queries = jnp.dot(normed, q_weight[layer], preferred_element_type=jnp.float32) + q_bias[layer].astype(jnp.float32)
        keyval = jnp.dot(normed, kv_weight[layer].reshape(D, KVH * 2 * HD), preferred_element_type=jnp.float32)
        keyval = keyval + kv_bias[layer].reshape(KVH * 2 * HD).astype(jnp.float32)
        queries = queries.reshape(MICRO, SEQ_TOK, QH, HD)
        keyval = keyval.reshape(MICRO, SEQ_TOK, KVH, 2 * HD)
        queries = rotate(queries, cosine, sine_tab).astype(jnp.bfloat16)
        key_rows = rotate(keyval[..., :HD], cosine, sine_tab).astype(jnp.bfloat16)
        value_rows = keyval[..., HD:].astype(jnp.bfloat16)
        key_heads = key_rows[:, :, head_group, :].astype(jnp.float32)
        value_heads = value_rows[:, :, head_group, :].astype(jnp.float32)
        scores = jnp.einsum('mqhd,mkhd->mhqk', queries.astype(jnp.float32), key_heads) / math.sqrt(HD)
        scores = jnp.where(causal[None, None], scores, -1e+30)
        row_max = lax.optimization_barrier(jnp.max(scores, axis=-1, keepdims=True))
        expo = jnp.exp(scores - row_max)
        weights_bf = (expo / lax.optimization_barrier(jnp.sum(expo, axis=-1, keepdims=True))).astype(jnp.bfloat16)
        context = jnp.einsum('mhqk,mkhd->mqhd', weights_bf.astype(jnp.float32), value_heads).astype(jnp.bfloat16)
        update = jnp.dot(context.reshape(MICRO * SEQ_TOK, QH * HD), out_weight[layer], preferred_element_type=jnp.float32)
        hidden = (residual + update).astype(jnp.bfloat16).reshape(MICRO, SEQ_TOK, D)
        collected.append(hidden.reshape(MICRO * SEQ_TOK, D))
    return jnp.stack(collected, axis=0)
```

```python
import functools
import math

import jax
import jax.numpy as jnp
import numpy as np
from jax import lax
from jax.experimental import pallas as pl
from jax.experimental.pallas import tpu as pltpu
from jax.sharding import PartitionSpec as P

MICRO = 2
EPS = 1e-06
THETA = 1000000.0
LANES = 128
MESH = pl.DeviceIdType.MESH


def tables(tok_count, head_size):
    half_size = head_size // 2
    frequency = np.float32(THETA) ** (
        -np.arange(half_size, dtype=np.float32) * np.float32(2.0) / np.float32(head_size)
    )
    angles = np.arange(tok_count, dtype=np.float32)[:, None] * frequency[None, :]
    cosine = np.concatenate([np.cos(angles), np.cos(angles)], axis=-1)
    signed_sine = np.concatenate([-np.sin(angles), np.sin(angles)], axis=-1)
    return cosine.astype(np.float32), signed_sine.astype(np.float32)


def rotate(values, cosine, signed_sine):
    return values * cosine + pltpu.roll(values, values.shape[1] // 2, 1) * signed_sine


def kernel(
    cfg,
    text,
    img,
    target,
    gain,
    q_hbm,
    q_bias,
    kv_hbm,
    kv_bias,
    out_hbm,
    cos_ref,
    sin_ref,
    out,
    w_all,
    w_out,
    rows,
    ctx,
    images,
    marks,
    gains,
    load_sem,
    z_send,
    z_recv,
    far_send,
    far_recv,
    fwd_send,
    fwd_recv,
    ctx_send,
    ctx_recv,
    gain_send,
    gain_recv,
    img_send,
    img_recv,
    mark_send,
    mark_recv,
):
    sections, seqs, tps, chunks = cfg
    members = seqs * tps
    sec = lax.axis_index("section")
    my_s = lax.axis_index("seq")
    my_t = lax.axis_index("tp")
    me = my_s * tps + my_t
    mate = {"seq": my_s, "tp": my_t + 1 - 2 * lax.rem(my_t, 2)}
    mate_t = mate["tp"]
    toks = text.shape[0] // MICRO
    width = text.shape[1]
    cw = width // chunks
    hd = q_hbm.shape[1]
    slots_own = img.shape[0]
    slots = slots_own * members // MICRO
    is_first = sec == 0

    loads = [
        pltpu.make_async_copy(q_hbm, w_all.at[:, pl.ds(0, hd)], load_sem.at[0]),
        pltpu.make_async_copy(kv_hbm, w_all.at[:, pl.ds(hd, 2 * hd)], load_sem.at[1]),
        pltpu.make_async_copy(out_hbm, w_out, load_sem.at[2]),
    ]
    for load in loads:
        load.start()

    def at_offset(ds, dt, sign=1, base_t=None):
        base = my_t if base_t is None else base_t
        s = lax.rem(my_s + sign * ds + seqs, seqs)
        t = lax.rem(base + sign * dt + tps, tps)
        return s, t

    offsets = [(ds, dt) for ds in range(seqs) for dt in range(tps) if (ds, dt) != (0, 0)]
    far = [(ds, dt) for ds in range(seqs) for dt in range(0, tps, 2) if (ds, dt) != (0, 0)]

    def remote(src, dst, send, recv, device):
        return pltpu.make_async_remote_copy(
            src_ref=src,
            dst_ref=dst,
            send_sem=send,
            recv_sem=recv,
            device_id=device,
            device_id_type=MESH,
        )

    barrier = pltpu.get_barrier_semaphore()
    for ds, dt in offsets:
        s, t = at_offset(ds, dt)
        pl.semaphore_signal(barrier, inc=1, device_id={"seq": s, "tp": t}, device_id_type=MESH)

    @pl.when(sec > 0)
    def _():
        pl.semaphore_signal(barrier, inc=1, device_id={"section": sec - 1}, device_id_type=MESH)

    for j in range(width // LANES):
        gains[me, j : j + 1, :] = gain[0:1, j * LANES : (j + 1) * LANES].astype(jnp.float32)
    lane = lax.broadcasted_iota(jnp.int32, (8, LANES), 1)
    row = lax.broadcasted_iota(jnp.int32, (8, LANES), 0)
    tile = jnp.full((8, LANES), -1, jnp.int32)
    for k in range(slots_own):
        spot = me * slots_own + k
        here = (row == lax.div(spot, slots)) & (lane == lax.rem(spot, slots))
        tile = jnp.where(here, target[k], tile)
    marks[me] = tile
    images[me] = img[:, pl.ds(pl.multiple_of(me * width, width), width)]

    @pl.when(sec == sections - 1)
    def _():
        pl.semaphore_wait(barrier, members - 1)

    @pl.when(sec < sections - 1)
    def _():
        pl.semaphore_wait(barrier, members)

    def img_copy(i):
        s, t = at_offset(*offsets[i])
        peer = s * tps + t
        cols = pl.ds(pl.multiple_of(peer * width, width), width)
        dev = {"seq": s, "tp": t}
        return (
            remote(img.at[:, cols], images.at[me], img_send.at[i], img_recv.at[i], dev),
            remote(marks.at[me], marks.at[me], mark_send.at[i], mark_recv.at[i], dev),
        )

    def gain_copy(i):
        s, t = at_offset(*offsets[i])
        return remote(
            gains.at[me], gains.at[me], gain_send.at[i], gain_recv.at[i], {"seq": s, "tp": t}
        )

    def source(i):
        s, t = at_offset(*offsets[i], sign=-1)
        return s * tps + t

    @pl.when(is_first)
    def _():
        for i in range(len(offsets)):
            for copy in img_copy(i):
                copy.start()

    for i in range(len(offsets)):
        gain_copy(i).start()

    @pl.when(is_first)
    def _():
        for i in range(len(offsets)):
            p = source(i)
            remote(
                marks.at[p], marks.at[p], mark_send.at[i], mark_recv.at[i], mate
            ).wait_recv()
            remote(
                images.at[p], images.at[p], img_send.at[i], img_recv.at[i], mate
            ).wait_recv()
        merged = marks[0]
        for p in range(1, members):
            merged = jnp.maximum(merged, marks[p])
        position = lax.broadcasted_iota(jnp.int32, (toks, slots), 0)
        per_mb = members // MICRO
        for m in range(MICRO):
            match = jnp.where(merged[m : m + 1, :slots] == position, 1.0, 0.0)
            stack = jnp.concatenate(
                [images[m * per_mb + p].astype(jnp.float32) for p in range(per_mb)], axis=0
            ).astype(jnp.bfloat16)
            placed = jnp.dot(
                match.astype(jnp.bfloat16), stack, preferred_element_type=jnp.float32
            )
            is_image = jnp.max(match, axis=1, keepdims=True) > 0.5
            plain = text[m * toks : (m + 1) * toks, :].astype(jnp.float32)
            rows[m, me] = jnp.where(is_image, placed, plain).astype(jnp.bfloat16)

    def cols_of(c):
        return pl.ds(c * cw, cw)

    def z_copy(m, c):
        return remote(
            out.at[0, pl.ds(m * toks, toks), cols_of(c)],
            rows.at[m, me, :, cols_of(c)],
            z_send.at[m, c],
            z_recv.at[m, c],
            {"section": lax.rem(sec + 1, sections)},
        )

    def own_to(m, c, i):
        s, t = at_offset(*far[i])
        ref = rows.at[m, me, :, cols_of(c)]
        return remote(
            ref, ref, far_send.at[m, c, i], far_recv.at[m, c, i], {"seq": s, "tp": t}
        )

    def far_piece(i):
        s, t = at_offset(*far[i], sign=-1)
        return s * tps + t

    def to_mate(m, c, i):
        piece = me if i == 0 else far_piece(i - 1)
        ref = rows.at[m, piece, :, cols_of(c)]
        return remote(ref, ref, fwd_send.at[m, c, i], fwd_recv.at[m, c, i], mate)

    def mate_piece(i):
        ds, dt = (0, 0) if i == 0 else far[i - 1]
        s, t = at_offset(ds, dt, sign=-1, base_t=mate_t)
        return s * tps + t

    def launch(m):
        for c in range(chunks):

            @pl.when(sec > 0)
            def _():
                z_copy(m, c).wait_recv()

            for i in range(len(far)):
                own_to(m, c, i).start()
            to_mate(m, c, 0).start()

    def piece_step(m, p, c, carry):
        total, squares = carry
        piece = rows[m, p, :, c * cw : (c + 1) * cw].astype(jnp.float32)
        first = c * cw // LANES
        scale = jnp.concatenate(
            [gains[p, pl.ds(first + j, 1), :] for j in range(cw // LANES)], axis=1
        )
        for j in range(cw // LANES):
            part = piece[:, j * LANES : (j + 1) * LANES]
            squares = squares + part * part
        weight = w_all[pl.ds(pl.multiple_of(p * width + c * cw, cw), cw), :]
        total = total + jnp.dot(
            (piece * scale).astype(jnp.bfloat16), weight, preferred_element_type=jnp.float32
        )
        return total, squares

    def project(m):
        carry = (
            jnp.zeros((toks, 3 * hd), jnp.float32),
            jnp.zeros((toks, LANES), jnp.float32),
        )
        for c in range(chunks):
            carry = piece_step(m, me, c, carry)
        for c in range(chunks):
            p = mate_piece(0)
            ref = rows.at[m, p, :, cols_of(c)]
            remote(ref, ref, fwd_send.at[m, c, 0], fwd_recv.at[m, c, 0], mate).wait_recv()
            carry = piece_step(m, p, c, carry)
        for c in range(chunks):
            for i in range(len(far)):
                p = far_piece(i)
                ref = rows.at[m, p, :, cols_of(c)]
                remote(
                    ref, ref, far_send.at[m, c, i], far_recv.at[m, c, i], mate
                ).wait_recv()
                to_mate(m, c, i + 1).start()
                carry = piece_step(m, p, c, carry)
            for i in range(len(far)):
                p = mate_piece(i + 1)
                ref = rows.at[m, p, :, cols_of(c)]
                remote(
                    ref, ref, fwd_send.at[m, c, i + 1], fwd_recv.at[m, c, i + 1], mate
                ).wait_recv()
                carry = piece_step(m, p, c, carry)
        return carry

    def ctx_copy(m, i):
        s, t = at_offset(*offsets[i])
        ref = ctx.at[m, :, pl.ds(pl.multiple_of(me * hd, hd), hd)]
        return remote(ref, ref, ctx_send.at[m, i], ctx_recv.at[m, i], {"seq": s, "tp": t})

    bias = jnp.concatenate([q_bias[...], kv_bias[...]], axis=1).astype(jnp.float32)
    cosine = cos_ref[...]
    signed_sine = sin_ref[...]
    query_at = lax.broadcasted_iota(jnp.int32, (toks, toks), 0)
    key_at = lax.broadcasted_iota(jnp.int32, (toks, toks), 1)

    def attend(m, carry):
        total, squares = carry
        mean = jnp.sum(squares, axis=1, keepdims=True) / (width * members)
        biased = total * lax.rsqrt(mean + EPS) + bias
        queries = rotate(biased[:, :hd], cosine, signed_sine).astype(jnp.bfloat16)
        keys = rotate(biased[:, hd : 2 * hd], cosine, signed_sine).astype(jnp.bfloat16)
        values = biased[:, 2 * hd :].astype(jnp.bfloat16)
        scores = lax.dot_general(
            queries, keys, (((1,), (1,)), ((), ())), preferred_element_type=jnp.float32
        )
        scores = jnp.where(query_at >= key_at, scores * (1.0 / math.sqrt(hd)), -1e30)
        expo = jnp.exp(scores - jnp.max(scores, axis=1, keepdims=True))
        probs = (expo / jnp.sum(expo, axis=1, keepdims=True)).astype(jnp.bfloat16)
        context = jnp.dot(probs, values, preferred_element_type=jnp.float32)
        ctx[m, :, pl.ds(pl.multiple_of(me * hd, hd), hd)] = context.astype(jnp.bfloat16)
        for i in range(len(offsets)):
            ctx_copy(m, i).start()

    def finish(m):
        for i in range(len(offsets)):
            p = source(i)
            ref = ctx.at[m, :, pl.ds(pl.multiple_of(p * hd, hd), hd)]
            remote(ref, ref, ctx_send.at[m, i], ctx_recv.at[m, i], mate).wait_recv()
        for c in range(chunks):
            update = jnp.dot(
                ctx[m], w_out[:, c * cw : (c + 1) * cw], preferred_element_type=jnp.float32
            )
            before = rows[m, me, :, c * cw : (c + 1) * cw].astype(jnp.float32)
            out[0, m * toks : (m + 1) * toks, c * cw : (c + 1) * cw] = (before + update).astype(
                jnp.bfloat16
            )

            @pl.when(sec < sections - 1)
            def _():
                z_copy(m, c).start()

    launch(0)
    for i in range(len(offsets)):
        p = source(i)
        remote(
            gains.at[p], gains.at[p], gain_send.at[i], gain_recv.at[i], mate
        ).wait_recv()
    loads[0].wait()
    loads[1].wait()
    attend(0, project(0))
    loads[2].wait()
    for m in range(MICRO):
        if m + 1 < MICRO:
            launch(m + 1)
        finish(m)
        if m + 1 < MICRO:
            attend(m + 1, project(m + 1))

    for m in range(MICRO):
        for c in range(chunks):
            for i in range(len(far)):
                own_to(m, c, i).wait_send()
            for i in range(len(far) + 1):
                to_mate(m, c, i).wait_send()

            @pl.when(sec < sections - 1)
            def _():
                z_copy(m, c).wait_send()

        for i in range(len(offsets)):
            ctx_copy(m, i).wait_send()
    for i in range(len(offsets)):
        gain_copy(i).wait_send()

    @pl.when(is_first)
    def _():
        for i in range(len(offsets)):
            for copy in img_copy(i):
                copy.wait_send()


def per_device(
    sizes,
    text_rows,
    image_rows,
    image_target,
    norm_gain,
    q_weight,
    q_bias,
    kv_weight,
    kv_bias,
    out_weight,
):
    sections, seqs, tps = sizes
    members = seqs * tps
    tok_count = text_rows.shape[0] // MICRO
    width = text_rows.shape[1]
    head_size = q_weight.shape[2]
    chunks = 2 if width >= 512 else 1
    features = width * members
    cosine, signed_sine = tables(tok_count, head_size)
    others = members - 1
    far = seqs * tps // 2 - 1
    vmem = pl.BlockSpec(memory_space=pltpu.VMEM)
    hbm = pl.BlockSpec(memory_space=pl.ANY)
    smem = pl.BlockSpec(memory_space=pltpu.SMEM)
    dma = pltpu.SemaphoreType.DMA
    bf16 = jnp.bfloat16
    return pl.pallas_call(
        functools.partial(kernel, (sections, seqs, tps, chunks)),
        out_shape=jax.ShapeDtypeStruct((1, MICRO * tok_count, width), bf16),
        in_specs=[vmem, vmem, smem, vmem, hbm, vmem, hbm, vmem, hbm, vmem, vmem],
        out_specs=vmem,
        scratch_shapes=[
            pltpu.VMEM((features, 3 * head_size), bf16),
            pltpu.VMEM((members * head_size, width), bf16),
            pltpu.VMEM((MICRO, members, tok_count, width), bf16),
            pltpu.VMEM((MICRO, tok_count, members * head_size), bf16),
            pltpu.VMEM((members, image_rows.shape[0], width), bf16),
            pltpu.VMEM((members, 8, LANES), jnp.int32),
            pltpu.VMEM((members, 8, LANES), jnp.float32),
            dma((3,)),
            dma((MICRO, chunks)),
            dma((MICRO, chunks)),
            dma((MICRO, chunks, far)),
            dma((MICRO, chunks, far)),
            dma((MICRO, chunks, far + 1)),
            dma((MICRO, chunks, far + 1)),
            dma((MICRO, others)),
            dma((MICRO, others)),
            dma((others,)),
            dma((others,)),
            dma((others,)),
            dma((others,)),
            dma((others,)),
            dma((others,)),
        ],
        compiler_params=pltpu.CompilerParams(
            collective_id=0, has_side_effects=True, vmem_limit_bytes=40 * 1024 * 1024
        ),
    )(
        text_rows,
        image_rows,
        image_target,
        norm_gain,
        q_weight[0],
        q_bias,
        kv_weight[0].reshape(features, 2 * head_size),
        kv_bias[0],
        out_weight[0],
        jnp.asarray(cosine),
        jnp.asarray(signed_sine),
    )


def solution(mesh):
    sizes = tuple(mesh.shape[axis] for axis in ("section", "seq", "tp"))
    in_specs = (
        P(None, ("seq", "tp")),
        P(("seq", "tp"), None),
        P(("seq", "tp")),
        P("section", ("seq", "tp")),
        P("section", None, ("seq", "tp")),
        P("section", ("seq", "tp")),
        P("section", None, "tp", None),
        P("section", "tp", None),
        P("section", None, ("seq", "tp")),
    )
    out_specs = P("section", None, ("seq", "tp"))
    return jax.shard_map(
        functools.partial(per_device, sizes),
        mesh=mesh,
        in_specs=in_specs,
        out_specs=out_specs,
        check_vma=False,
    )
```

```python
import functools
import math

import jax
import jax.numpy as jnp
import numpy as np
from jax import lax
from jax.experimental import pallas as pl
from jax.experimental.pallas import tpu as pltpu
from jax.sharding import PartitionSpec as P

MICRO = 2
EPS = 1e-06
THETA = 1000000.0
LANES = 128
MESH = pl.DeviceIdType.MESH


def tables(tok_count, head_size):
    half_size = head_size // 2
    frequency = np.float32(THETA) ** (
        -np.arange(half_size, dtype=np.float32) * np.float32(2.0) / np.float32(head_size)
    )
    angles = np.arange(tok_count, dtype=np.float32)[:, None] * frequency[None, :]
    cosine = np.concatenate([np.cos(angles), np.cos(angles)], axis=-1)
    signed_sine = np.concatenate([-np.sin(angles), np.sin(angles)], axis=-1)
    return cosine.astype(np.float32), signed_sine.astype(np.float32)


def rotate(values, cosine, signed_sine):
    return values * cosine + pltpu.roll(values, values.shape[1] // 2, 1) * signed_sine


def kernel(
    cfg,
    text_hbm,
    img,
    target_hbm,
    gain_hbm,
    q_hbm,
    q_bias_hbm,
    kv_hbm,
    kv_bias_hbm,
    out_hbm,
    table_hbm,
    out,
    text,
    target,
    gain,
    q_bias,
    kv_bias,
    table,
    w_all,
    w_out,
    rows,
    ctx,
    images,
    marks,
    gains,
    load_sem,
    z_send,
    z_recv,
    far_send,
    far_recv,
    fwd_send,
    fwd_recv,
    ctx_send,
    ctx_recv,
    gain_send,
    gain_recv,
    img_send,
    img_recv,
    mark_send,
    mark_recv,
):
    sections, seqs, tps, chunks = cfg
    members = seqs * tps
    sec = lax.axis_index("section")
    my_s = lax.axis_index("seq")
    my_t = lax.axis_index("tp")
    me = my_s * tps + my_t
    mate = {"seq": my_s, "tp": my_t + 1 - 2 * lax.rem(my_t, 2)}
    mate_t = mate["tp"]
    toks = text_hbm.shape[0] // MICRO
    width = text_hbm.shape[1]
    cw = width // chunks
    hd = q_hbm.shape[1]
    slots_own = img.shape[0]
    slots = slots_own * members // MICRO
    is_first = sec == 0

    def at_offset(ds, dt, sign=1, base_t=None):
        base = my_t if base_t is None else base_t
        s = lax.rem(my_s + sign * ds + seqs, seqs)
        t = lax.rem(base + sign * dt + tps, tps)
        return s, t

    offsets = [(ds, dt) for ds in range(seqs) for dt in range(tps) if (ds, dt) != (0, 0)]
    far = [(ds, dt) for ds in range(seqs) for dt in range(0, tps, 2) if (ds, dt) != (0, 0)]

    def remote(src, dst, send, recv, device):
        return pltpu.make_async_remote_copy(
            src_ref=src,
            dst_ref=dst,
            send_sem=send,
            recv_sem=recv,
            device_id=device,
            device_id_type=MESH,
        )

    barrier = pltpu.get_barrier_semaphore()
    for ds, dt in offsets:
        s, t = at_offset(ds, dt)
        pl.semaphore_signal(barrier, inc=1, device_id={"seq": s, "tp": t}, device_id_type=MESH)

    @pl.when(sec > 0)
    def _():
        pl.semaphore_signal(barrier, inc=1, device_id={"section": sec - 1}, device_id_type=MESH)

    own_cols = pl.ds(pl.multiple_of(me * width, width), width)
    early = [
        pltpu.make_async_copy(target_hbm, target, load_sem.at[0]),
        pltpu.make_async_copy(gain_hbm, gain, load_sem.at[1]),
        pltpu.make_async_copy(img.at[:, own_cols], images.at[me], load_sem.at[2]),
        pltpu.make_async_copy(text_hbm, text, load_sem.at[3]),
    ]
    loads = [
        pltpu.make_async_copy(q_hbm, w_all.at[:, pl.ds(0, hd)], load_sem.at[4]),
        pltpu.make_async_copy(kv_hbm, w_all.at[:, pl.ds(hd, 2 * hd)], load_sem.at[5]),
        pltpu.make_async_copy(q_bias_hbm, q_bias, load_sem.at[6]),
        pltpu.make_async_copy(kv_bias_hbm, kv_bias, load_sem.at[7]),
        pltpu.make_async_copy(table_hbm, table, load_sem.at[8]),
        pltpu.make_async_copy(out_hbm, w_out, load_sem.at[9]),
    ]
    for load in early + loads:
        load.start()
    for load in early:
        load.wait()

    for j in range(width // LANES):
        gains[me, j : j + 1, :] = gain[0:1, j * LANES : (j + 1) * LANES].astype(jnp.float32)
    lane = lax.broadcasted_iota(jnp.int32, (8, LANES), 1)
    row = lax.broadcasted_iota(jnp.int32, (8, LANES), 0)
    tile = jnp.full((8, LANES), -1, jnp.int32)
    for k in range(slots_own):
        spot = me * slots_own + k
        here = (row == lax.div(spot, slots)) & (lane == lax.rem(spot, slots))
        tile = jnp.where(here, target[k], tile)
    marks[me] = tile

    @pl.when(sec == sections - 1)
    def _():
        pl.semaphore_wait(barrier, members - 1)

    @pl.when(sec < sections - 1)
    def _():
        pl.semaphore_wait(barrier, members)

    def img_copy(i):
        s, t = at_offset(*offsets[i])
        peer = s * tps + t
        cols = pl.ds(pl.multiple_of(peer * width, width), width)
        dev = {"seq": s, "tp": t}
        return (
            remote(marks.at[me], marks.at[me], mark_send.at[i], mark_recv.at[i], dev),
            remote(img.at[:, cols], images.at[me], img_send.at[i], img_recv.at[me], dev),
        )

    def gain_copy(i):
        s, t = at_offset(*offsets[i])
        return remote(
            gains.at[me], gains.at[me], gain_send.at[i], gain_recv.at[i], {"seq": s, "tp": t}
        )

    def source(i):
        s, t = at_offset(*offsets[i], sign=-1)
        return s * tps + t

    @pl.when(is_first)
    def _():
        for i in range(len(offsets)):
            for copy in img_copy(i):
                copy.start()

    for i in range(len(offsets)):
        gain_copy(i).start()

    per_mb = members // MICRO
    position = lax.broadcasted_iota(jnp.int32, (toks, slots), 0)

    def embed(m):
        merged = marks[0]
        for p in range(1, members):
            merged = jnp.maximum(merged, marks[p])
        match = jnp.where(merged[m : m + 1, :slots] == position, 1.0, 0.0)
        for p in range(m * per_mb, (m + 1) * per_mb):

            @pl.when(me != p)
            def _():
                remote(
                    images.at[p], images.at[p], img_send.at[0], img_recv.at[p], mate
                ).wait_recv()

        stack = jnp.concatenate(
            [images[m * per_mb + p].astype(jnp.float32) for p in range(per_mb)], axis=0
        ).astype(jnp.bfloat16)
        placed = jnp.dot(match.astype(jnp.bfloat16), stack, preferred_element_type=jnp.float32)
        is_image = jnp.max(match, axis=1, keepdims=True) > 0.5
        plain = text[m * toks : (m + 1) * toks, :].astype(jnp.float32)
        rows[m, me] = jnp.where(is_image, placed, plain).astype(jnp.bfloat16)

    @pl.when(is_first)
    def _():
        for i in range(len(offsets)):
            p = source(i)
            remote(
                marks.at[p], marks.at[p], mark_send.at[i], mark_recv.at[i], mate
            ).wait_recv()
        embed(0)

    def cols_of(c):
        return pl.ds(c * cw, cw)

    def z_copy(m, c):
        return remote(
            out.at[0, pl.ds(m * toks, toks), cols_of(c)],
            rows.at[m, me, :, cols_of(c)],
            z_send.at[m, c],
            z_recv.at[m, c],
            {"section": lax.rem(sec + 1, sections)},
        )

    relayed = seqs == 2 and tps == 4 and chunks == 2
    across = far.index((0, 2)) if relayed else None
    along = far.index((1, 0)) if relayed else None
    corner = far.index((1, 2)) if relayed else None

    def direct(i):
        return not relayed or i != corner

    def relay(m, c):
        got, to = (across, along) if c == 0 else (along, across)
        s, t = at_offset(*far[to])
        ref = rows.at[m, far_piece(got), :, cols_of(c)]
        return remote(
            ref,
            ref,
            far_send.at[m, c, corner],
            far_recv.at[m, c, corner],
            {"seq": s, "tp": t},
        )

    def own_to(m, c, i):
        s, t = at_offset(*far[i])
        ref = rows.at[m, me, :, cols_of(c)]
        return remote(
            ref, ref, far_send.at[m, c, i], far_recv.at[m, c, i], {"seq": s, "tp": t}
        )

    def far_piece(i):
        s, t = at_offset(*far[i], sign=-1)
        return s * tps + t

    def to_mate(m, c, i):
        piece = me if i == 0 else far_piece(i - 1)
        ref = rows.at[m, piece, :, cols_of(c)]
        return remote(ref, ref, fwd_send.at[m, c, i], fwd_recv.at[m, c, i], mate)

    def mate_piece(i):
        ds, dt = (0, 0) if i == 0 else far[i - 1]
        s, t = at_offset(ds, dt, sign=-1, base_t=mate_t)
        return s * tps + t

    def launch(m):
        for c in range(chunks):

            @pl.when(sec > 0)
            def _():
                z_copy(m, c).wait_recv()

            for i in range(len(far)):
                if direct(i):
                    own_to(m, c, i).start()
            to_mate(m, c, 0).start()

    def piece_step(m, p, c, carry):
        total, squares = carry
        piece = rows[m, p, :, c * cw : (c + 1) * cw].astype(jnp.float32)
        first = c * cw // LANES
        scale = jnp.concatenate(
            [gains[p, pl.ds(first + j, 1), :] for j in range(cw // LANES)], axis=1
        )
        for j in range(cw // LANES):
            part = piece[:, j * LANES : (j + 1) * LANES]
            squares = squares + part * part
        weight = w_all[pl.ds(pl.multiple_of(p * width + c * cw, cw), cw), :]
        total = total + jnp.dot(
            (piece * scale).astype(jnp.bfloat16), weight, preferred_element_type=jnp.float32
        )
        return total, squares

    def take_far(m, c, i, carry):
        p = far_piece(i)
        ref = rows.at[m, p, :, cols_of(c)]
        remote(ref, ref, far_send.at[m, c, i], far_recv.at[m, c, i], mate).wait_recv()
        if relayed and i == (across if c == 0 else along):
            relay(m, c).start()
        to_mate(m, c, i + 1).start()
        return piece_step(m, p, c, carry)

    def take_mate(m, c, i, carry):
        p = mate_piece(i)
        ref = rows.at[m, p, :, cols_of(c)]
        remote(ref, ref, fwd_send.at[m, c, i], fwd_recv.at[m, c, i], mate).wait_recv()
        return piece_step(m, p, c, carry)

    def project_near(m):
        carry = (
            jnp.zeros((toks, 3 * hd), jnp.float32),
            jnp.zeros((toks, LANES), jnp.float32),
        )
        for c in range(chunks):
            carry = piece_step(m, me, c, carry)
        for c in range(chunks):
            carry = take_mate(m, c, 0, carry)
        return carry

    def project_far(m, carry):
        late = [i for i in range(len(far)) if not direct(i)]
        soon = [i for i in range(len(far)) if direct(i)]
        for group in (soon, late):
            for c in range(chunks):
                order = group if c == 0 else group[::-1]
                for i in order:
                    carry = take_far(m, c, i, carry)
                if group is late:
                    continue
                for i in order:
                    carry = take_mate(m, c, i + 1, carry)
        for c in range(chunks):
            for i in late:
                carry = take_mate(m, c, i + 1, carry)
        return carry

    def ctx_copy(m, i):
        s, t = at_offset(*offsets[i])
        ref = ctx.at[m, :, pl.ds(pl.multiple_of(me * hd, hd), hd)]
        return remote(ref, ref, ctx_send.at[m, i], ctx_recv.at[m, i], {"seq": s, "tp": t})

    query_at = lax.broadcasted_iota(jnp.int32, (toks, toks), 0)
    key_at = lax.broadcasted_iota(jnp.int32, (toks, toks), 1)

    def attend(m, carry):
        total, squares = carry
        bias = jnp.concatenate([q_bias[...], kv_bias[...]], axis=1).astype(jnp.float32)
        cosine = table[0]
        signed_sine = table[1]
        mean = jnp.sum(squares, axis=1, keepdims=True) / (width * members)
        biased = total * lax.rsqrt(mean + EPS) + bias
        queries = rotate(biased[:, :hd], cosine, signed_sine).astype(jnp.bfloat16)
        keys = rotate(biased[:, hd : 2 * hd], cosine, signed_sine).astype(jnp.bfloat16)
        values = biased[:, 2 * hd :].astype(jnp.bfloat16)
        scores = lax.dot_general(
            queries, keys, (((1,), (1,)), ((), ())), preferred_element_type=jnp.float32
        )
        scores = jnp.where(query_at >= key_at, scores * (1.0 / math.sqrt(hd)), -1e30)
        expo = jnp.exp(scores - jnp.max(scores, axis=1, keepdims=True))
        probs = (expo / jnp.sum(expo, axis=1, keepdims=True)).astype(jnp.bfloat16)
        context = jnp.dot(probs, values, preferred_element_type=jnp.float32)
        ctx[m, :, pl.ds(pl.multiple_of(me * hd, hd), hd)] = context.astype(jnp.bfloat16)
        for i in range(len(offsets)):
            ctx_copy(m, i).start()

    def finish(m):
        for i in range(len(offsets)):
            p = source(i)
            ref = ctx.at[m, :, pl.ds(pl.multiple_of(p * hd, hd), hd)]
            remote(ref, ref, ctx_send.at[m, i], ctx_recv.at[m, i], mate).wait_recv()
        for c in range(chunks):
            update = jnp.dot(
                ctx[m], w_out[:, c * cw : (c + 1) * cw], preferred_element_type=jnp.float32
            )
            before = rows[m, me, :, c * cw : (c + 1) * cw].astype(jnp.float32)
            out[0, m * toks : (m + 1) * toks, c * cw : (c + 1) * cw] = (before + update).astype(
                jnp.bfloat16
            )

            @pl.when(sec < sections - 1)
            def _():
                z_copy(m, c).start()

    launch(0)
    for i in range(len(offsets)):
        p = source(i)
        remote(
            gains.at[p], gains.at[p], gain_send.at[i], gain_recv.at[i], mate
        ).wait_recv()
    loads[0].wait()
    loads[1].wait()

    @pl.when(is_first)
    def _():
        for m in range(1, MICRO):
            embed(m)

    carry = project_far(0, project_near(0))
    for load in loads[2:]:
        load.wait()
    for m in range(MICRO):
        if m + 1 < MICRO:

            @pl.when(is_first)
            def _():
                launch(m + 1)

        attend(m, carry)
        if m + 1 < MICRO:

            @pl.when(sec > 0)
            def _():
                launch(m + 1)

            carry = project_near(m + 1)
        finish(m)
        if m + 1 < MICRO:
            carry = project_far(m + 1, carry)

    for m in range(MICRO):
        for c in range(chunks):
            for i in range(len(far)):
                if direct(i):
                    own_to(m, c, i).wait_send()
            if relayed:
                relay(m, c).wait_send()
            for i in range(len(far) + 1):
                to_mate(m, c, i).wait_send()

            @pl.when(sec < sections - 1)
            def _():
                z_copy(m, c).wait_send()

        for i in range(len(offsets)):
            ctx_copy(m, i).wait_send()
    for i in range(len(offsets)):
        gain_copy(i).wait_send()

    @pl.when(is_first)
    def _():
        for i in range(len(offsets)):
            for copy in img_copy(i):
                copy.wait_send()


def per_device(
    sizes,
    text_rows,
    image_rows,
    image_target,
    norm_gain,
    q_weight,
    q_bias,
    kv_weight,
    kv_bias,
    out_weight,
):
    sections, seqs, tps = sizes
    members = seqs * tps
    tok_count = text_rows.shape[0] // MICRO
    width = text_rows.shape[1]
    head_size = q_weight.shape[2]
    chunks = 2 if width >= 512 else 1
    features = width * members
    cosine, signed_sine = tables(tok_count, head_size)
    others = members - 1
    far = seqs * tps // 2 - 1
    vmem = pl.BlockSpec(memory_space=pltpu.VMEM)
    hbm = pl.BlockSpec(memory_space=pltpu.HBM)
    dma = pltpu.SemaphoreType.DMA
    bf16 = jnp.bfloat16
    return pl.pallas_call(
        functools.partial(kernel, (sections, seqs, tps, chunks)),
        out_shape=jax.ShapeDtypeStruct((1, MICRO * tok_count, width), bf16),
        in_specs=[hbm] * 10,
        out_specs=vmem,
        scratch_shapes=[
            pltpu.VMEM(text_rows.shape, bf16),
            pltpu.SMEM(image_target.shape, jnp.int32),
            pltpu.VMEM(norm_gain.shape, bf16),
            pltpu.VMEM(q_bias.shape, bf16),
            pltpu.VMEM(kv_bias.shape[1:], bf16),
            pltpu.VMEM((2, tok_count, head_size), jnp.float32),
            pltpu.VMEM((features, 3 * head_size), bf16),
            pltpu.VMEM((members * head_size, width), bf16),
            pltpu.VMEM((MICRO, members, tok_count, width), bf16),
            pltpu.VMEM((MICRO, tok_count, members * head_size), bf16),
            pltpu.VMEM((members, image_rows.shape[0], width), bf16),
            pltpu.VMEM((members, 8, LANES), jnp.int32),
            pltpu.VMEM((members, 8, LANES), jnp.float32),
            dma((10,)),
            dma((MICRO, chunks)),
            dma((MICRO, chunks)),
            dma((MICRO, chunks, far)),
            dma((MICRO, chunks, far)),
            dma((MICRO, chunks, far + 1)),
            dma((MICRO, chunks, far + 1)),
            dma((MICRO, others)),
            dma((MICRO, others)),
            dma((others,)),
            dma((others,)),
            dma((others,)),
            dma((members,)),
            dma((others,)),
            dma((others,)),
        ],
        compiler_params=pltpu.CompilerParams(
            collective_id=0, has_side_effects=True, vmem_limit_bytes=60 * 1024 * 1024
        ),
    )(
        text_rows,
        image_rows,
        image_target,
        norm_gain,
        q_weight[0],
        q_bias,
        kv_weight[0].reshape(features, 2 * head_size),
        kv_bias[0],
        out_weight[0],
        jnp.asarray(np.stack([cosine, signed_sine])),
    )


def solution(mesh):
    sizes = tuple(mesh.shape[axis] for axis in ("section", "seq", "tp"))
    in_specs = (
        P(None, ("seq", "tp")),
        P(("seq", "tp"), None),
        P(("seq", "tp")),
        P("section", ("seq", "tp")),
        P("section", None, ("seq", "tp")),
        P("section", ("seq", "tp")),
        P("section", None, "tp", None),
        P("section", "tp", None),
        P("section", None, ("seq", "tp")),
    )
    out_specs = P("section", None, ("seq", "tp"))
    return jax.shard_map(
        functools.partial(per_device, sizes),
        mesh=mesh,
        in_specs=in_specs,
        out_specs=out_specs,
        check_vma=False,
    )
```

```python
import functools
import math

import jax
import jax.numpy as jnp
import numpy as np
from jax import lax
from jax.experimental import pallas as pl
from jax.experimental.pallas import tpu as pltpu
from jax.sharding import PartitionSpec as P

MICRO = 2
EPS = 1e-06
THETA = 1000000.0
LANES = 128
MESH = pl.DeviceIdType.MESH


def tables(tok_count, head_size):
    half_size = head_size // 2
    frequency = np.float32(THETA) ** (
        -np.arange(half_size, dtype=np.float32) * np.float32(2.0) / np.float32(head_size)
    )
    angles = np.arange(tok_count, dtype=np.float32)[:, None] * frequency[None, :]
    cosine = np.concatenate([np.cos(angles), np.cos(angles)], axis=-1)
    signed_sine = np.concatenate([-np.sin(angles), np.sin(angles)], axis=-1)
    return cosine.astype(np.float32), signed_sine.astype(np.float32)


def rotate(values, cosine, signed_sine):
    return values * cosine + pltpu.roll(values, values.shape[1] // 2, 1) * signed_sine


def kernel(
    cfg,
    text_hbm,
    img,
    target_hbm,
    gain_hbm,
    q_hbm,
    q_bias_hbm,
    kv_hbm,
    kv_bias_hbm,
    out_hbm,
    table_hbm,
    out,
    text,
    target,
    gain,
    q_bias,
    kv_bias,
    table,
    w_all,
    w_out,
    rows,
    ctx,
    images,
    marks,
    gains,
    load_sem,
    z_send,
    z_recv,
    far_send,
    far_recv,
    fwd_send,
    fwd_recv,
    ctx_send,
    ctx_recv,
    gain_send,
    gain_recv,
    img_send,
    img_recv,
    mark_send,
    mark_recv,
):
    sections, seqs, tps, chunks = cfg
    members = seqs * tps
    sec = lax.axis_index("section")
    my_s = lax.axis_index("seq")
    my_t = lax.axis_index("tp")
    me = my_s * tps + my_t
    mate = {"seq": my_s, "tp": my_t + 1 - 2 * lax.rem(my_t, 2)}
    mate_t = mate["tp"]
    toks = text_hbm.shape[0] // MICRO
    width = text_hbm.shape[1]
    cw = width // chunks
    hd = q_hbm.shape[1]
    slots_own = img.shape[0]
    slots = slots_own * members // MICRO
    is_first = sec == 0

    def at_offset(ds, dt, sign=1, base_t=None):
        base = my_t if base_t is None else base_t
        s = lax.rem(my_s + sign * ds + seqs, seqs)
        t = lax.rem(base + sign * dt + tps, tps)
        return s, t

    offsets = [(ds, dt) for ds in range(seqs) for dt in range(tps) if (ds, dt) != (0, 0)]
    far = [(ds, dt) for ds in range(seqs) for dt in range(0, tps, 2) if (ds, dt) != (0, 0)]

    def remote(src, dst, send, recv, device):
        return pltpu.make_async_remote_copy(
            src_ref=src,
            dst_ref=dst,
            send_sem=send,
            recv_sem=recv,
            device_id=device,
            device_id_type=MESH,
        )

    barrier = pltpu.get_barrier_semaphore()
    for ds, dt in offsets:
        s, t = at_offset(ds, dt)
        pl.semaphore_signal(barrier, inc=1, device_id={"seq": s, "tp": t}, device_id_type=MESH)

    @pl.when(sec > 0)
    def _():
        pl.semaphore_signal(barrier, inc=1, device_id={"section": sec - 1}, device_id_type=MESH)

    own_cols = pl.ds(pl.multiple_of(me * width, width), width)
    early = [
        pltpu.make_async_copy(target_hbm, target, load_sem.at[0]),
        pltpu.make_async_copy(gain_hbm, gain, load_sem.at[1]),
        pltpu.make_async_copy(img.at[:, own_cols], images.at[me], load_sem.at[2]),
        pltpu.make_async_copy(text_hbm, text, load_sem.at[3]),
    ]
    loads = [
        pltpu.make_async_copy(q_hbm, w_all.at[:, pl.ds(0, hd)], load_sem.at[4]),
        pltpu.make_async_copy(kv_hbm, w_all.at[:, pl.ds(hd, 2 * hd)], load_sem.at[5]),
        pltpu.make_async_copy(q_bias_hbm, q_bias, load_sem.at[6]),
        pltpu.make_async_copy(kv_bias_hbm, kv_bias, load_sem.at[7]),
        pltpu.make_async_copy(table_hbm, table, load_sem.at[8]),
        pltpu.make_async_copy(out_hbm, w_out, load_sem.at[9]),
    ]
    for load in early + loads:
        load.start()
    for load in early:
        load.wait()

    for j in range(width // LANES):
        gains[me, j : j + 1, :] = gain[0:1, j * LANES : (j + 1) * LANES].astype(jnp.float32)
    lane = lax.broadcasted_iota(jnp.int32, (8, LANES), 1)
    row = lax.broadcasted_iota(jnp.int32, (8, LANES), 0)
    tile = jnp.full((8, LANES), -1, jnp.int32)
    for k in range(slots_own):
        spot = me * slots_own + k
        here = (row == lax.div(spot, slots)) & (lane == lax.rem(spot, slots))
        tile = jnp.where(here, target[k], tile)
    marks[me] = tile

    @pl.when(sec == sections - 1)
    def _():
        pl.semaphore_wait(barrier, members - 1)

    @pl.when(sec < sections - 1)
    def _():
        pl.semaphore_wait(barrier, members)

    def img_copy(i):
        s, t = at_offset(*offsets[i])
        peer = s * tps + t
        cols = pl.ds(pl.multiple_of(peer * width, width), width)
        dev = {"seq": s, "tp": t}
        return (
            remote(marks.at[me], marks.at[me], mark_send.at[i], mark_recv.at[i], dev),
            remote(img.at[:, cols], images.at[me], img_send.at[i], img_recv.at[me], dev),
        )

    def gain_copy(i):
        s, t = at_offset(*offsets[i])
        return remote(
            gains.at[me], gains.at[me], gain_send.at[i], gain_recv.at[i], {"seq": s, "tp": t}
        )

    def source(i):
        s, t = at_offset(*offsets[i], sign=-1)
        return s * tps + t

    @pl.when(is_first)
    def _():
        for i in range(len(offsets)):
            for copy in img_copy(i):
                copy.start()

    for i in range(len(offsets)):
        gain_copy(i).start()

    per_mb = members // MICRO
    position = lax.broadcasted_iota(jnp.int32, (toks, slots), 0)

    def embed(m):
        merged = marks[0]
        for p in range(1, members):
            merged = jnp.maximum(merged, marks[p])
        match = jnp.where(merged[m : m + 1, :slots] == position, 1.0, 0.0)
        for p in range(m * per_mb, (m + 1) * per_mb):

            @pl.when(me != p)
            def _():
                remote(
                    images.at[p], images.at[p], img_send.at[0], img_recv.at[p], mate
                ).wait_recv()

        stack = jnp.concatenate(
            [images[m * per_mb + p].astype(jnp.float32) for p in range(per_mb)], axis=0
        ).astype(jnp.bfloat16)
        placed = jnp.dot(match.astype(jnp.bfloat16), stack, preferred_element_type=jnp.float32)
        is_image = jnp.max(match, axis=1, keepdims=True) > 0.5
        plain = text[m * toks : (m + 1) * toks, :].astype(jnp.float32)
        rows[m, me] = jnp.where(is_image, placed, plain).astype(jnp.bfloat16)

    @pl.when(is_first)
    def _():
        for i in range(len(offsets)):
            p = source(i)
            remote(
                marks.at[p], marks.at[p], mark_send.at[i], mark_recv.at[i], mate
            ).wait_recv()
        embed(0)

    def cols_of(c):
        return pl.ds(c * cw, cw)

    def z_copy(m, c):
        return remote(
            out.at[0, pl.ds(m * toks, toks), cols_of(c)],
            rows.at[m, me, :, cols_of(c)],
            z_send.at[m, c],
            z_recv.at[m, c],
            {"section": lax.rem(sec + 1, sections)},
        )

    relayed = seqs == 2 and tps == 4 and chunks == 2
    across = far.index((0, 2)) if relayed else None
    along = far.index((1, 0)) if relayed else None
    corner = far.index((1, 2)) if relayed else None

    def direct(i):
        return not relayed or i != corner

    def relay(m, c):
        got, to = (across, along) if c == 0 else (along, across)
        s, t = at_offset(*far[to])
        ref = rows.at[m, far_piece(got), :, cols_of(c)]
        return remote(
            ref,
            ref,
            far_send.at[m, c, corner],
            far_recv.at[m, c, corner],
            {"seq": s, "tp": t},
        )

    def own_to(m, c, i):
        s, t = at_offset(*far[i])
        ref = rows.at[m, me, :, cols_of(c)]
        return remote(
            ref, ref, far_send.at[m, c, i], far_recv.at[m, c, i], {"seq": s, "tp": t}
        )

    def far_piece(i):
        s, t = at_offset(*far[i], sign=-1)
        return s * tps + t

    def to_mate(m, c, i):
        piece = me if i == 0 else far_piece(i - 1)
        ref = rows.at[m, piece, :, cols_of(c)]
        return remote(ref, ref, fwd_send.at[m, c, i], fwd_recv.at[m, c, i], mate)

    def mate_piece(i):
        ds, dt = (0, 0) if i == 0 else far[i - 1]
        s, t = at_offset(ds, dt, sign=-1, base_t=mate_t)
        return s * tps + t

    def launch(m):
        for c in range(chunks):

            @pl.when(sec > 0)
            def _():
                z_copy(m, c).wait_recv()

            for i in range(len(far)):
                if direct(i):
                    own_to(m, c, i).start()
            to_mate(m, c, 0).start()

    def piece_step(m, p, c, carry):
        total, squares = carry
        piece = rows[m, p, :, c * cw : (c + 1) * cw].astype(jnp.float32)
        first = c * cw // LANES
        scale = jnp.concatenate(
            [gains[p, pl.ds(first + j, 1), :] for j in range(cw // LANES)], axis=1
        )
        for j in range(cw // LANES):
            part = piece[:, j * LANES : (j + 1) * LANES]
            squares = squares + part * part
        weight = w_all[pl.ds(pl.multiple_of(p * width + c * cw, cw), cw), :]
        total = total + jnp.dot(
            (piece * scale).astype(jnp.bfloat16), weight, preferred_element_type=jnp.float32
        )
        return total, squares

    def take_far(m, c, i, carry):
        p = far_piece(i)
        ref = rows.at[m, p, :, cols_of(c)]
        remote(ref, ref, far_send.at[m, c, i], far_recv.at[m, c, i], mate).wait_recv()
        if relayed and i == (across if c == 0 else along):
            relay(m, c).start()
        to_mate(m, c, i + 1).start()
        return piece_step(m, p, c, carry)

    def take_mate(m, c, i, carry):
        p = mate_piece(i)
        ref = rows.at[m, p, :, cols_of(c)]
        remote(ref, ref, fwd_send.at[m, c, i], fwd_recv.at[m, c, i], mate).wait_recv()
        return piece_step(m, p, c, carry)

    def project_near(m):
        carry = (
            jnp.zeros((toks, 3 * hd), jnp.float32),
            jnp.zeros((toks, LANES), jnp.float32),
        )
        for c in range(chunks):
            carry = piece_step(m, me, c, carry)
        for c in range(chunks):
            carry = take_mate(m, c, 0, carry)
        return carry

    def project_far(m, carry):
        late = [i for i in range(len(far)) if not direct(i)]
        soon = [i for i in range(len(far)) if direct(i)]
        for group in (soon, late):
            for c in range(chunks):
                order = group if c == 0 else group[::-1]
                for i in order:
                    carry = take_far(m, c, i, carry)
                if group is late:
                    continue
                for i in order:
                    carry = take_mate(m, c, i + 1, carry)
        for c in range(chunks):
            for i in late:
                carry = take_mate(m, c, i + 1, carry)
        return carry

    def ctx_copy(m, i):
        s, t = at_offset(*offsets[i])
        ref = ctx.at[m, :, pl.ds(pl.multiple_of(me * hd, hd), hd)]
        return remote(ref, ref, ctx_send.at[m, i], ctx_recv.at[m, i], {"seq": s, "tp": t})

    query_at = lax.broadcasted_iota(jnp.int32, (toks, toks), 0)
    key_at = lax.broadcasted_iota(jnp.int32, (toks, toks), 1)

    def attend(m, carry):
        total, squares = carry
        bias = jnp.concatenate([q_bias[...], kv_bias[...]], axis=1).astype(jnp.float32)
        cosine = table[0]
        signed_sine = table[1]
        mean = jnp.sum(squares, axis=1, keepdims=True) / (width * members)
        biased = total * lax.rsqrt(mean + EPS) + bias
        queries = rotate(biased[:, :hd], cosine, signed_sine).astype(jnp.bfloat16)
        keys = rotate(biased[:, hd : 2 * hd], cosine, signed_sine).astype(jnp.bfloat16)
        values = biased[:, 2 * hd :].astype(jnp.bfloat16)
        scores = lax.dot_general(
            queries, keys, (((1,), (1,)), ((), ())), preferred_element_type=jnp.float32
        )
        scores = jnp.where(query_at >= key_at, scores * (1.0 / math.sqrt(hd)), -1e30)
        expo = jnp.exp(scores - jnp.max(scores, axis=1, keepdims=True))
        probs = (expo / jnp.sum(expo, axis=1, keepdims=True)).astype(jnp.bfloat16)
        context = jnp.dot(probs, values, preferred_element_type=jnp.float32)
        ctx[m, :, pl.ds(pl.multiple_of(me * hd, hd), hd)] = context.astype(jnp.bfloat16)
        for i in range(len(offsets)):
            ctx_copy(m, i).start()

    def finish(m):
        for i in range(len(offsets)):
            p = source(i)
            ref = ctx.at[m, :, pl.ds(pl.multiple_of(p * hd, hd), hd)]
            remote(ref, ref, ctx_send.at[m, i], ctx_recv.at[m, i], mate).wait_recv()
        for c in range(chunks):
            update = jnp.dot(
                ctx[m], w_out[:, c * cw : (c + 1) * cw], preferred_element_type=jnp.float32
            )
            before = rows[m, me, :, c * cw : (c + 1) * cw].astype(jnp.float32)
            out[0, m * toks : (m + 1) * toks, c * cw : (c + 1) * cw] = (before + update).astype(
                jnp.bfloat16
            )

            @pl.when(sec < sections - 1)
            def _():
                z_copy(m, c).start()

    launch(0)
    for i in range(len(offsets)):
        p = source(i)
        remote(
            gains.at[p], gains.at[p], gain_send.at[i], gain_recv.at[i], mate
        ).wait_recv()
    loads[0].wait()
    loads[1].wait()

    @pl.when(is_first)
    def _():
        for m in range(1, MICRO):
            embed(m)

    carry = project_far(0, project_near(0))
    for load in loads[2:]:
        load.wait()
    for m in range(MICRO):
        if m + 1 < MICRO:

            @pl.when(is_first)
            def _():
                launch(m + 1)

        attend(m, carry)
        finish(m)
        if m + 1 < MICRO:

            @pl.when(sec > 0)
            def _():
                launch(m + 1)

            carry = project_far(m + 1, project_near(m + 1))

    for m in range(MICRO):
        for c in range(chunks):
            for i in range(len(far)):
                if direct(i):
                    own_to(m, c, i).wait_send()
            if relayed:
                relay(m, c).wait_send()
            for i in range(len(far) + 1):
                to_mate(m, c, i).wait_send()

            @pl.when(sec < sections - 1)
            def _():
                z_copy(m, c).wait_send()

        for i in range(len(offsets)):
            ctx_copy(m, i).wait_send()
    for i in range(len(offsets)):
        gain_copy(i).wait_send()

    @pl.when(is_first)
    def _():
        for i in range(len(offsets)):
            for copy in img_copy(i):
                copy.wait_send()


def per_device(
    sizes,
    text_rows,
    image_rows,
    image_target,
    norm_gain,
    q_weight,
    q_bias,
    kv_weight,
    kv_bias,
    out_weight,
):
    sections, seqs, tps = sizes
    members = seqs * tps
    tok_count = text_rows.shape[0] // MICRO
    width = text_rows.shape[1]
    head_size = q_weight.shape[2]
    chunks = 2 if width >= 512 else 1
    features = width * members
    cosine, signed_sine = tables(tok_count, head_size)
    others = members - 1
    far = seqs * tps // 2 - 1
    vmem = pl.BlockSpec(memory_space=pltpu.VMEM)
    hbm = pl.BlockSpec(memory_space=pltpu.HBM)
    dma = pltpu.SemaphoreType.DMA
    bf16 = jnp.bfloat16
    return pl.pallas_call(
        functools.partial(kernel, (sections, seqs, tps, chunks)),
        out_shape=jax.ShapeDtypeStruct((1, MICRO * tok_count, width), bf16),
        in_specs=[hbm] * 10,
        out_specs=vmem,
        scratch_shapes=[
            pltpu.VMEM(text_rows.shape, bf16),
            pltpu.SMEM(image_target.shape, jnp.int32),
            pltpu.VMEM(norm_gain.shape, bf16),
            pltpu.VMEM(q_bias.shape, bf16),
            pltpu.VMEM(kv_bias.shape[1:], bf16),
            pltpu.VMEM((2, tok_count, head_size), jnp.float32),
            pltpu.VMEM((features, 3 * head_size), bf16),
            pltpu.VMEM((members * head_size, width), bf16),
            pltpu.VMEM((MICRO, members, tok_count, width), bf16),
            pltpu.VMEM((MICRO, tok_count, members * head_size), bf16),
            pltpu.VMEM((members, image_rows.shape[0], width), bf16),
            pltpu.VMEM((members, 8, LANES), jnp.int32),
            pltpu.VMEM((members, 8, LANES), jnp.float32),
            dma((10,)),
            dma((MICRO, chunks)),
            dma((MICRO, chunks)),
            dma((MICRO, chunks, far)),
            dma((MICRO, chunks, far)),
            dma((MICRO, chunks, far + 1)),
            dma((MICRO, chunks, far + 1)),
            dma((MICRO, others)),
            dma((MICRO, others)),
            dma((others,)),
            dma((others,)),
            dma((others,)),
            dma((members,)),
            dma((others,)),
            dma((others,)),
        ],
        compiler_params=pltpu.CompilerParams(
            collective_id=0, has_side_effects=True, vmem_limit_bytes=60 * 1024 * 1024
        ),
    )(
        text_rows,
        image_rows,
        image_target,
        norm_gain,
        q_weight[0],
        q_bias,
        kv_weight[0].reshape(features, 2 * head_size),
        kv_bias[0],
        out_weight[0],
        jnp.asarray(np.stack([cosine, signed_sine])),
    )


def solution(mesh):
    sizes = tuple(mesh.shape[axis] for axis in ("section", "seq", "tp"))
    in_specs = (
        P(None, ("seq", "tp")),
        P(("seq", "tp"), None),
        P(("seq", "tp")),
        P("section", ("seq", "tp")),
        P("section", None, ("seq", "tp")),
        P("section", ("seq", "tp")),
        P("section", None, "tp", None),
        P("section", "tp", None),
        P("section", None, ("seq", "tp")),
    )
    out_specs = P("section", None, ("seq", "tp"))
    return jax.shard_map(
        functools.partial(per_device, sizes),
        mesh=mesh,
        in_specs=in_specs,
        out_specs=out_specs,
        check_vma=False,
    )
```

```python
import functools
import math

import jax
import jax.numpy as jnp
import numpy as np
from jax import lax
from jax.experimental import pallas as pl
from jax.experimental.pallas import tpu as pltpu
from jax.sharding import PartitionSpec as P

MICRO = 2
EPS = 1e-06
THETA = 1000000.0
LANES = 128
MESH = pl.DeviceIdType.MESH


def tables(tok_count, head_size):
    half_size = head_size // 2
    frequency = np.float32(THETA) ** (
        -np.arange(half_size, dtype=np.float32) * np.float32(2.0) / np.float32(head_size)
    )
    angles = np.arange(tok_count, dtype=np.float32)[:, None] * frequency[None, :]
    cosine = np.concatenate([np.cos(angles), np.cos(angles)], axis=-1)
    signed_sine = np.concatenate([-np.sin(angles), np.sin(angles)], axis=-1)
    return cosine.astype(np.float32), signed_sine.astype(np.float32)


def rotate(values, cosine, signed_sine):
    return values * cosine + pltpu.roll(values, values.shape[1] // 2, 1) * signed_sine


def kernel(
    cfg,
    text_hbm,
    img,
    target_hbm,
    gain_hbm,
    q_hbm,
    q_bias_hbm,
    kv_hbm,
    kv_bias_hbm,
    out_hbm,
    table_hbm,
    out,
    text,
    target,
    gain,
    q_bias,
    kv_bias,
    table,
    w_all,
    w_out,
    rows,
    ctx,
    part_out,
    part_in,
    images,
    marks,
    gains,
    load_sem,
    z_send,
    z_recv,
    far_send,
    far_recv,
    part_send,
    part_recv,
    w_send,
    w_recv,
    ctx_send,
    ctx_recv,
    gain_send,
    gain_recv,
    img_send,
    img_recv,
    mark_send,
    mark_recv,
):
    sections, seqs, tps, chunks = cfg
    members = seqs * tps
    sec = lax.axis_index("section")
    my_s = lax.axis_index("seq")
    my_t = lax.axis_index("tp")
    me = my_s * tps + my_t
    mate = {"seq": my_s, "tp": my_t + 1 - 2 * lax.rem(my_t, 2)}
    mate_t = mate["tp"]
    pairs = tps // 2
    half = seqs * pairs
    own = my_s * pairs + lax.div(my_t, 2)
    toks = text_hbm.shape[0] // MICRO
    width = text_hbm.shape[1]
    cw = width // chunks
    hd = q_hbm.shape[1]
    slots_own = img.shape[0]
    slots = slots_own * members // MICRO
    is_first = sec == 0

    def at_offset(ds, dt, sign=1, base_t=None):
        base = my_t if base_t is None else base_t
        s = lax.rem(my_s + sign * ds + seqs, seqs)
        t = lax.rem(base + sign * dt + tps, tps)
        return s, t

    offsets = [(ds, dt) for ds in range(seqs) for dt in range(tps) if (ds, dt) != (0, 0)]
    far = [(ds, dt) for ds in range(seqs) for dt in range(0, tps, 2) if (ds, dt) != (0, 0)]

    def remote(src, dst, send, recv, device):
        return pltpu.make_async_remote_copy(
            src_ref=src,
            dst_ref=dst,
            send_sem=send,
            recv_sem=recv,
            device_id=device,
            device_id_type=MESH,
        )

    barrier = pltpu.get_barrier_semaphore()
    for ds, dt in offsets:
        s, t = at_offset(ds, dt)
        pl.semaphore_signal(barrier, inc=1, device_id={"seq": s, "tp": t}, device_id_type=MESH)

    @pl.when(sec > 0)
    def _():
        pl.semaphore_signal(barrier, inc=1, device_id={"section": sec - 1}, device_id_type=MESH)

    own_cols = pl.ds(pl.multiple_of(me * width, width), width)
    early = [
        pltpu.make_async_copy(target_hbm, target, load_sem.at[0]),
        pltpu.make_async_copy(gain_hbm, gain, load_sem.at[1]),
        pltpu.make_async_copy(img.at[:, own_cols], images.at[me], load_sem.at[2]),
        pltpu.make_async_copy(text_hbm, text, load_sem.at[3]),
    ]
    loads = [
        pltpu.make_async_copy(q_bias_hbm, q_bias, load_sem.at[4]),
        pltpu.make_async_copy(kv_bias_hbm, kv_bias, load_sem.at[5]),
        pltpu.make_async_copy(table_hbm, table, load_sem.at[6]),
        pltpu.make_async_copy(out_hbm, w_out, load_sem.at[7]),
    ]
    weights = []
    for k in range(half):
        p = lax.div(k, pairs) * tps + lax.rem(k, pairs) * 2 + lax.rem(my_t, 2)
        at = pl.ds(pl.multiple_of(p * width, width), width)
        to = pl.ds(k * width, width)
        weights += [
            pltpu.make_async_copy(q_hbm.at[at, :], w_all.at[to, pl.ds(0, hd)], load_sem.at[8 + 2 * k]),
            pltpu.make_async_copy(
                kv_hbm.at[at, :], w_all.at[to, pl.ds(hd, 2 * hd)], load_sem.at[9 + 2 * k]
            ),
        ]
    for load in early + weights + loads:
        load.start()
    for load in early:
        load.wait()

    for j in range(width // LANES):
        gains[own, j : j + 1, :] = gain[0:1, j * LANES : (j + 1) * LANES].astype(jnp.float32)
    lane = lax.broadcasted_iota(jnp.int32, (8, LANES), 1)
    row = lax.broadcasted_iota(jnp.int32, (8, LANES), 0)
    tile = jnp.full((8, LANES), -1, jnp.int32)
    for k in range(slots_own):
        spot = me * slots_own + k
        here = (row == lax.div(spot, slots)) & (lane == lax.rem(spot, slots))
        tile = jnp.where(here, target[k], tile)
    marks[me] = tile

    @pl.when(sec == sections - 1)
    def _():
        pl.semaphore_wait(barrier, members - 1)

    @pl.when(sec < sections - 1)
    def _():
        pl.semaphore_wait(barrier, members)

    def img_copy(i):
        s, t = at_offset(*offsets[i])
        peer = s * tps + t
        cols = pl.ds(pl.multiple_of(peer * width, width), width)
        dev = {"seq": s, "tp": t}
        return (
            remote(marks.at[me], marks.at[me], mark_send.at[i], mark_recv.at[i], dev),
            remote(img.at[:, cols], images.at[me], img_send.at[i], img_recv.at[me], dev),
        )

    def gain_copy(i):
        s, t = at_offset(*far[i])
        return remote(
            gains.at[own], gains.at[own], gain_send.at[i], gain_recv.at[i], {"seq": s, "tp": t}
        )

    def weight_copies():
        copies = []
        for k in range(half):
            p = lax.div(k, pairs) * tps + lax.rem(k, pairs) * 2 + lax.rem(mate_t, 2)
            at = pl.ds(pl.multiple_of(p * width, width), width)
            to = pl.ds(k * width, width)
            copies += [
                remote(
                    q_hbm.at[at, :],
                    w_all.at[to, pl.ds(3 * hd, hd)],
                    w_send.at[2 * k],
                    w_recv.at[2 * k],
                    mate,
                ),
                remote(
                    kv_hbm.at[at, :],
                    w_all.at[to, pl.ds(4 * hd, 2 * hd)],
                    w_send.at[2 * k + 1],
                    w_recv.at[2 * k + 1],
                    mate,
                ),
            ]
        return copies

    def source(i):
        s, t = at_offset(*offsets[i], sign=-1)
        return s * tps + t

    @pl.when(is_first)
    def _():
        for i in range(len(offsets)):
            for copy in img_copy(i):
                copy.start()

    for i in range(len(far)):
        gain_copy(i).start()
    for copy in weight_copies():
        copy.start()

    per_mb = members // MICRO
    position = lax.broadcasted_iota(jnp.int32, (toks, slots), 0)

    def embed(m):
        merged = marks[0]
        for p in range(1, members):
            merged = jnp.maximum(merged, marks[p])
        match = jnp.where(merged[m : m + 1, :slots] == position, 1.0, 0.0)
        for p in range(m * per_mb, (m + 1) * per_mb):

            @pl.when(me != p)
            def _():
                remote(
                    images.at[p], images.at[p], img_send.at[0], img_recv.at[p], mate
                ).wait_recv()

        stack = jnp.concatenate(
            [images[m * per_mb + p].astype(jnp.float32) for p in range(per_mb)], axis=0
        ).astype(jnp.bfloat16)
        placed = jnp.dot(match.astype(jnp.bfloat16), stack, preferred_element_type=jnp.float32)
        is_image = jnp.max(match, axis=1, keepdims=True) > 0.5
        plain = text[m * toks : (m + 1) * toks, :].astype(jnp.float32)
        rows[m, own] = jnp.where(is_image, placed, plain).astype(jnp.bfloat16)

    @pl.when(is_first)
    def _():
        for i in range(len(offsets)):
            p = source(i)
            remote(
                marks.at[p], marks.at[p], mark_send.at[i], mark_recv.at[i], mate
            ).wait_recv()
        embed(0)

    def cols_of(c):
        return pl.ds(c * cw, cw)

    def z_copy(m, c):
        return remote(
            out.at[0, pl.ds(m * toks, toks), cols_of(c)],
            rows.at[m, own, :, cols_of(c)],
            z_send.at[m, c],
            z_recv.at[m, c],
            {"section": lax.rem(sec + 1, sections)},
        )

    def own_to(m, c, i):
        s, t = at_offset(*far[i])
        ref = rows.at[m, own, :, cols_of(c)]
        return remote(
            ref, ref, far_send.at[m, c, i], far_recv.at[m, c, i], {"seq": s, "tp": t}
        )

    def far_block(i):
        s, t = at_offset(*far[i], sign=-1)
        return s * pairs + lax.div(t, 2)

    def launch(m):
        for c in range(chunks):

            @pl.when(sec > 0)
            def _():
                z_copy(m, c).wait_recv()

            for i in range(len(far)):
                own_to(m, c, i).start()

    def block_step(m, k, c, carry):
        total, squares = carry
        piece = rows[m, k, :, c * cw : (c + 1) * cw].astype(jnp.float32)
        first = c * cw // LANES
        scale = jnp.concatenate(
            [gains[k, pl.ds(first + j, 1), :] for j in range(cw // LANES)], axis=1
        )
        for j in range(cw // LANES):
            part = piece[:, j * LANES : (j + 1) * LANES]
            squares = squares + part * part
        weight = w_all[pl.ds(pl.multiple_of(k * width + c * cw, cw), cw), :]
        total = total + jnp.dot(
            (piece * scale).astype(jnp.bfloat16), weight, preferred_element_type=jnp.float32
        )
        return total, squares

    def part_copy(m):
        return remote(part_out.at[m], part_in.at[m], part_send.at[m], part_recv.at[m], mate)

    def project(m):
        carry = (
            jnp.zeros((toks, 6 * hd), jnp.float32),
            jnp.zeros((toks, LANES), jnp.float32),
        )
        for c in range(chunks):
            carry = block_step(m, own, c, carry)
        for c in range(chunks):
            for i in range(len(far)):
                k = far_block(i)
                ref = rows.at[m, k, :, cols_of(c)]
                remote(
                    ref, ref, far_send.at[m, c, i], far_recv.at[m, c, i], mate
                ).wait_recv()
                carry = block_step(m, k, c, carry)
        total, squares = carry
        part_out[m, :, : 3 * hd] = total[:, 3 * hd :]
        part_out[m, :, 3 * hd :] = squares
        part_copy(m).start()
        part_copy(m).wait_recv()
        total = total[:, : 3 * hd] + part_in[m, :, : 3 * hd]
        return total, squares + part_in[m, :, 3 * hd :]

    def ctx_copy(m, i):
        s, t = at_offset(*offsets[i])
        ref = ctx.at[m, :, pl.ds(pl.multiple_of(me * hd, hd), hd)]
        return remote(ref, ref, ctx_send.at[m, i], ctx_recv.at[m, i], {"seq": s, "tp": t})

    query_at = lax.broadcasted_iota(jnp.int32, (toks, toks), 0)
    key_at = lax.broadcasted_iota(jnp.int32, (toks, toks), 1)

    def attend(m, carry):
        total, squares = carry
        bias = jnp.concatenate([q_bias[...], kv_bias[...]], axis=1).astype(jnp.float32)
        cosine = table[0]
        signed_sine = table[1]
        mean = jnp.sum(squares, axis=1, keepdims=True) / (width * members)
        biased = total * lax.rsqrt(mean + EPS) + bias
        queries = rotate(biased[:, :hd], cosine, signed_sine).astype(jnp.bfloat16)
        keys = rotate(biased[:, hd : 2 * hd], cosine, signed_sine).astype(jnp.bfloat16)
        values = biased[:, 2 * hd :].astype(jnp.bfloat16)
        scores = lax.dot_general(
            queries, keys, (((1,), (1,)), ((), ())), preferred_element_type=jnp.float32
        )
        scores = jnp.where(query_at >= key_at, scores * (1.0 / math.sqrt(hd)), -1e30)
        expo = jnp.exp(scores - jnp.max(scores, axis=1, keepdims=True))
        probs = (expo / jnp.sum(expo, axis=1, keepdims=True)).astype(jnp.bfloat16)
        context = jnp.dot(probs, values, preferred_element_type=jnp.float32)
        ctx[m, :, pl.ds(pl.multiple_of(me * hd, hd), hd)] = context.astype(jnp.bfloat16)
        for i in range(len(offsets)):
            ctx_copy(m, i).start()

    def finish(m):
        for i in range(len(offsets)):
            p = source(i)
            ref = ctx.at[m, :, pl.ds(pl.multiple_of(p * hd, hd), hd)]
            remote(ref, ref, ctx_send.at[m, i], ctx_recv.at[m, i], mate).wait_recv()
        for c in range(chunks):
            update = jnp.dot(
                ctx[m], w_out[:, c * cw : (c + 1) * cw], preferred_element_type=jnp.float32
            )
            before = rows[m, own, :, c * cw : (c + 1) * cw].astype(jnp.float32)
            out[0, m * toks : (m + 1) * toks, c * cw : (c + 1) * cw] = (before + update).astype(
                jnp.bfloat16
            )

            @pl.when(sec < sections - 1)
            def _():
                z_copy(m, c).start()

    launch(0)
    for i in range(len(far)):
        k = far_block(i)
        remote(
            gains.at[k], gains.at[k], gain_send.at[i], gain_recv.at[i], mate
        ).wait_recv()

    @pl.when(is_first)
    def _():
        for m in range(1, MICRO):
            embed(m)

    for load in weights:
        load.wait()
    for copy in weight_copies():
        copy.wait_recv()
    carry = project(0)
    for load in loads:
        load.wait()
    for m in range(MICRO):
        if m + 1 < MICRO:

            @pl.when(is_first)
            def _():
                launch(m + 1)

        attend(m, carry)
        if m + 1 < MICRO:

            @pl.when(sec > 0)
            def _():
                launch(m + 1)

        finish(m)
        if m + 1 < MICRO:
            carry = project(m + 1)

    for copy in weight_copies():
        copy.wait_send()
    for m in range(MICRO):
        part_copy(m).wait_send()
        for c in range(chunks):
            for i in range(len(far)):
                own_to(m, c, i).wait_send()

            @pl.when(sec < sections - 1)
            def _():
                z_copy(m, c).wait_send()

        for i in range(len(offsets)):
            ctx_copy(m, i).wait_send()
    for i in range(len(far)):
        gain_copy(i).wait_send()

    @pl.when(is_first)
    def _():
        for i in range(len(offsets)):
            for copy in img_copy(i):
                copy.wait_send()


def per_device(
    sizes,
    text_rows,
    image_rows,
    image_target,
    norm_gain,
    q_weight,
    q_bias,
    kv_weight,
    kv_bias,
    out_weight,
):
    sections, seqs, tps = sizes
    members = seqs * tps
    tok_count = text_rows.shape[0] // MICRO
    width = text_rows.shape[1]
    head_size = q_weight.shape[2]
    chunks = 2 if width >= 512 else 1
    features = width * members
    cosine, signed_sine = tables(tok_count, head_size)
    others = members - 1
    half = members // 2
    far = half - 1
    vmem = pl.BlockSpec(memory_space=pltpu.VMEM)
    hbm = pl.BlockSpec(memory_space=pltpu.HBM)
    dma = pltpu.SemaphoreType.DMA
    bf16 = jnp.bfloat16
    return pl.pallas_call(
        functools.partial(kernel, (sections, seqs, tps, chunks)),
        out_shape=jax.ShapeDtypeStruct((1, MICRO * tok_count, width), bf16),
        in_specs=[hbm] * 10,
        out_specs=vmem,
        scratch_shapes=[
            pltpu.VMEM(text_rows.shape, bf16),
            pltpu.SMEM(image_target.shape, jnp.int32),
            pltpu.VMEM(norm_gain.shape, bf16),
            pltpu.VMEM(q_bias.shape, bf16),
            pltpu.VMEM(kv_bias.shape[1:], bf16),
            pltpu.VMEM((2, tok_count, head_size), jnp.float32),
            pltpu.VMEM((half * width, 6 * head_size), bf16),
            pltpu.VMEM((members * head_size, width), bf16),
            pltpu.VMEM((MICRO, half, tok_count, width), bf16),
            pltpu.VMEM((MICRO, tok_count, members * head_size), bf16),
            pltpu.VMEM((MICRO, tok_count, 3 * head_size + LANES), jnp.float32),
            pltpu.VMEM((MICRO, tok_count, 3 * head_size + LANES), jnp.float32),
            pltpu.VMEM((members, image_rows.shape[0], width), bf16),
            pltpu.VMEM((members, 8, LANES), jnp.int32),
            pltpu.VMEM((half, 8, LANES), jnp.float32),
            dma((8 + 2 * half,)),
            dma((MICRO, chunks)),
            dma((MICRO, chunks)),
            dma((MICRO, chunks, far)),
            dma((MICRO, chunks, far)),
            dma((MICRO,)),
            dma((MICRO,)),
            dma((2 * half,)),
            dma((2 * half,)),
            dma((MICRO, others)),
            dma((MICRO, others)),
            dma((far,)),
            dma((far,)),
            dma((others,)),
            dma((members,)),
            dma((others,)),
            dma((others,)),
        ],
        compiler_params=pltpu.CompilerParams(
            collective_id=0, has_side_effects=True, vmem_limit_bytes=60 * 1024 * 1024
        ),
    )(
        text_rows,
        image_rows,
        image_target,
        norm_gain,
        q_weight[0],
        q_bias,
        kv_weight[0].reshape(features, 2 * head_size),
        kv_bias[0],
        out_weight[0],
        jnp.asarray(np.stack([cosine, signed_sine])),
    )


def solution(mesh):
    sizes = tuple(mesh.shape[axis] for axis in ("section", "seq", "tp"))
    in_specs = (
        P(None, ("seq", "tp")),
        P(("seq", "tp"), None),
        P(("seq", "tp")),
        P("section", ("seq", "tp")),
        P("section", None, ("seq", "tp")),
        P("section", ("seq", "tp")),
        P("section", None, "tp", None),
        P("section", "tp", None),
        P("section", None, ("seq", "tp")),
    )
    out_specs = P("section", None, ("seq", "tp"))
    return jax.shard_map(
        functools.partial(per_device, sizes),
        mesh=mesh,
        in_specs=in_specs,
        out_specs=out_specs,
        check_vma=False,
    )
```

```python
import functools
import math

import jax
import jax.numpy as jnp
import numpy as np
from jax import lax
from jax.experimental import pallas as pl
from jax.experimental.pallas import tpu as pltpu
from jax.sharding import PartitionSpec as P

MICRO = 2
EPS = 1e-06
THETA = 1000000.0
LANES = 128
MESH = pl.DeviceIdType.MESH


def tables(tok_count, head_size):
    half_size = head_size // 2
    frequency = np.float32(THETA) ** (
        -np.arange(half_size, dtype=np.float32) * np.float32(2.0) / np.float32(head_size)
    )
    angles = np.arange(tok_count, dtype=np.float32)[:, None] * frequency[None, :]
    cosine = np.concatenate([np.cos(angles), np.cos(angles)], axis=-1)
    signed_sine = np.concatenate([-np.sin(angles), np.sin(angles)], axis=-1)
    return cosine.astype(np.float32), signed_sine.astype(np.float32)


def rotate(values, cosine, signed_sine):
    return values * cosine + pltpu.roll(values, values.shape[1] // 2, 1) * signed_sine


def kernel(
    cfg,
    text_hbm,
    img,
    target_hbm,
    gain_hbm,
    q_hbm,
    q_bias_hbm,
    kv_hbm,
    kv_bias_hbm,
    out_hbm,
    table_hbm,
    out,
    text,
    target,
    gain,
    q_bias,
    kv_bias,
    table,
    w_all,
    w_out,
    rows,
    ctx,
    part_out,
    part_in,
    images,
    marks,
    gains,
    load_sem,
    z_send,
    z_recv,
    far_send,
    far_recv,
    part_send,
    part_recv,
    w_send,
    w_recv,
    ctx_send,
    ctx_recv,
    gain_send,
    gain_recv,
    img_send,
    img_recv,
    mark_send,
    mark_recv,
):
    sections, seqs, tps, chunks = cfg
    members = seqs * tps
    sec = lax.axis_index("section")
    my_s = lax.axis_index("seq")
    my_t = lax.axis_index("tp")
    me = my_s * tps + my_t
    mate = {"seq": my_s, "tp": my_t + 1 - 2 * lax.rem(my_t, 2)}
    mate_t = mate["tp"]
    pairs = tps // 2
    half = seqs * pairs
    own = my_s * pairs + lax.div(my_t, 2)
    toks = text_hbm.shape[0] // MICRO
    width = text_hbm.shape[1]
    cw = width // chunks
    hd = q_hbm.shape[1]
    slots_own = img.shape[0]
    slots = slots_own * members // MICRO
    is_first = sec == 0

    def at_offset(ds, dt, sign=1, base_t=None):
        base = my_t if base_t is None else base_t
        s = lax.rem(my_s + sign * ds + seqs, seqs)
        t = lax.rem(base + sign * dt + tps, tps)
        return s, t

    offsets = [(ds, dt) for ds in range(seqs) for dt in range(tps) if (ds, dt) != (0, 0)]
    far = [(ds, dt) for ds in range(seqs) for dt in range(0, tps, 2) if (ds, dt) != (0, 0)]

    def remote(src, dst, send, recv, device):
        return pltpu.make_async_remote_copy(
            src_ref=src,
            dst_ref=dst,
            send_sem=send,
            recv_sem=recv,
            device_id=device,
            device_id_type=MESH,
        )

    barrier = pltpu.get_barrier_semaphore()
    for ds, dt in offsets:
        s, t = at_offset(ds, dt)
        pl.semaphore_signal(barrier, inc=1, device_id={"seq": s, "tp": t}, device_id_type=MESH)

    @pl.when(sec > 0)
    def _():
        pl.semaphore_signal(barrier, inc=1, device_id={"section": sec - 1}, device_id_type=MESH)

    own_cols = pl.ds(pl.multiple_of(me * width, width), width)
    early = [
        pltpu.make_async_copy(target_hbm, target, load_sem.at[0]),
        pltpu.make_async_copy(gain_hbm, gain, load_sem.at[1]),
        pltpu.make_async_copy(img.at[:, own_cols], images.at[me], load_sem.at[2]),
        pltpu.make_async_copy(text_hbm, text, load_sem.at[3]),
    ]
    loads = [
        pltpu.make_async_copy(q_bias_hbm, q_bias, load_sem.at[4]),
        pltpu.make_async_copy(kv_bias_hbm, kv_bias, load_sem.at[5]),
        pltpu.make_async_copy(table_hbm, table, load_sem.at[6]),
        pltpu.make_async_copy(out_hbm, w_out, load_sem.at[7]),
    ]
    weights = []
    for k in range(half):
        p = lax.div(k, pairs) * tps + lax.rem(k, pairs) * 2 + lax.rem(my_t, 2)
        at = pl.ds(pl.multiple_of(p * width, width), width)
        to = pl.ds(k * width, width)
        weights += [
            pltpu.make_async_copy(q_hbm.at[at, :], w_all.at[to, pl.ds(0, hd)], load_sem.at[8 + 2 * k]),
            pltpu.make_async_copy(
                kv_hbm.at[at, :], w_all.at[to, pl.ds(hd, 2 * hd)], load_sem.at[9 + 2 * k]
            ),
        ]
    for load in early + weights + loads:
        load.start()
    for load in early:
        load.wait()

    for j in range(width // LANES):
        gains[own, j : j + 1, :] = gain[0:1, j * LANES : (j + 1) * LANES].astype(jnp.float32)
    lane = lax.broadcasted_iota(jnp.int32, (8, LANES), 1)
    row = lax.broadcasted_iota(jnp.int32, (8, LANES), 0)
    tile = jnp.full((8, LANES), -1, jnp.int32)
    for k in range(slots_own):
        spot = me * slots_own + k
        here = (row == lax.div(spot, slots)) & (lane == lax.rem(spot, slots))
        tile = jnp.where(here, target[k], tile)
    marks[me] = tile

    @pl.when(sec == sections - 1)
    def _():
        pl.semaphore_wait(barrier, members - 1)

    @pl.when(sec < sections - 1)
    def _():
        pl.semaphore_wait(barrier, members)

    def img_copy(i):
        s, t = at_offset(*offsets[i])
        peer = s * tps + t
        cols = pl.ds(pl.multiple_of(peer * width, width), width)
        dev = {"seq": s, "tp": t}
        return (
            remote(marks.at[me], marks.at[me], mark_send.at[i], mark_recv.at[i], dev),
            remote(img.at[:, cols], images.at[me], img_send.at[i], img_recv.at[me], dev),
        )

    def gain_copy(i):
        s, t = at_offset(*far[i])
        return remote(
            gains.at[own], gains.at[own], gain_send.at[i], gain_recv.at[i], {"seq": s, "tp": t}
        )

    def weight_copies():
        copies = []
        for k in range(half):
            p = lax.div(k, pairs) * tps + lax.rem(k, pairs) * 2 + lax.rem(mate_t, 2)
            at = pl.ds(pl.multiple_of(p * width, width), width)
            to = pl.ds(k * width, width)
            copies += [
                remote(
                    q_hbm.at[at, :],
                    w_all.at[to, pl.ds(3 * hd, hd)],
                    w_send.at[2 * k],
                    w_recv.at[2 * k],
                    mate,
                ),
                remote(
                    kv_hbm.at[at, :],
                    w_all.at[to, pl.ds(4 * hd, 2 * hd)],
                    w_send.at[2 * k + 1],
                    w_recv.at[2 * k + 1],
                    mate,
                ),
            ]
        return copies

    def source(i):
        s, t = at_offset(*offsets[i], sign=-1)
        return s * tps + t

    @pl.when(is_first)
    def _():
        for i in range(len(offsets)):
            for copy in img_copy(i):
                copy.start()

    for i in range(len(far)):
        gain_copy(i).start()
    for copy in weight_copies():
        copy.start()

    per_mb = members // MICRO
    position = lax.broadcasted_iota(jnp.int32, (toks, slots), 0)

    def embed(m):
        merged = marks[0]
        for p in range(1, members):
            merged = jnp.maximum(merged, marks[p])
        match = jnp.where(merged[m : m + 1, :slots] == position, 1.0, 0.0)
        for p in range(m * per_mb, (m + 1) * per_mb):

            @pl.when(me != p)
            def _():
                remote(
                    images.at[p], images.at[p], img_send.at[0], img_recv.at[p], mate
                ).wait_recv()

        stack = jnp.concatenate(
            [images[m * per_mb + p].astype(jnp.float32) for p in range(per_mb)], axis=0
        ).astype(jnp.bfloat16)
        placed = jnp.dot(match.astype(jnp.bfloat16), stack, preferred_element_type=jnp.float32)
        is_image = jnp.max(match, axis=1, keepdims=True) > 0.5
        plain = text[m * toks : (m + 1) * toks, :].astype(jnp.float32)
        rows[m, own] = jnp.where(is_image, placed, plain).astype(jnp.bfloat16)

    @pl.when(is_first)
    def _():
        for i in range(len(offsets)):
            p = source(i)
            remote(
                marks.at[p], marks.at[p], mark_send.at[i], mark_recv.at[i], mate
            ).wait_recv()
        embed(0)

    def cols_of(c):
        return pl.ds(c * cw, cw)

    def z_copy(m, c):
        return remote(
            out.at[0, pl.ds(m * toks, toks), cols_of(c)],
            rows.at[m, own, :, cols_of(c)],
            z_send.at[m, c],
            z_recv.at[m, c],
            {"section": lax.rem(sec + 1, sections)},
        )

    def own_to(m, c, i):
        s, t = at_offset(*far[i])
        ref = rows.at[m, own, :, cols_of(c)]
        return remote(
            ref, ref, far_send.at[m, c, i], far_recv.at[m, c, i], {"seq": s, "tp": t}
        )

    def far_block(i):
        s, t = at_offset(*far[i], sign=-1)
        return s * pairs + lax.div(t, 2)

    def launch(m):
        for c in range(chunks):

            @pl.when(sec > 0)
            def _():
                z_copy(m, c).wait_recv()

            for i in range(len(far)):
                own_to(m, c, i).start()

    def block_step(m, k, c, carry):
        total, squares = carry
        piece = rows[m, k, :, c * cw : (c + 1) * cw].astype(jnp.float32)
        first = c * cw // LANES
        scale = jnp.concatenate(
            [gains[k, pl.ds(first + j, 1), :] for j in range(cw // LANES)], axis=1
        )
        for j in range(cw // LANES):
            part = piece[:, j * LANES : (j + 1) * LANES]
            squares = squares + part * part
        weight = w_all[pl.ds(pl.multiple_of(k * width + c * cw, cw), cw), :]
        total = total + jnp.dot(
            (piece * scale).astype(jnp.bfloat16), weight, preferred_element_type=jnp.float32
        )
        return total, squares

    def part_copy(m):
        return remote(part_out.at[m], part_in.at[m], part_send.at[m], part_recv.at[m], mate)

    def take(m, c, carry):
        for i in range(len(far)):
            k = far_block(i)
            ref = rows.at[m, k, :, cols_of(c)]
            remote(ref, ref, far_send.at[m, c, i], far_recv.at[m, c, i], mate).wait_recv()
            carry = block_step(m, k, c, carry)
        return carry

    def project_first(m):
        carry = (
            jnp.zeros((toks, 6 * hd), jnp.float32),
            jnp.zeros((toks, LANES), jnp.float32),
        )
        for c in range(chunks):
            carry = block_step(m, own, c, carry)
        return take(m, 0, carry)

    def project_rest(m, carry):
        for c in range(1, chunks):
            carry = take(m, c, carry)
        total, squares = carry
        part_out[m, :, : 3 * hd] = total[:, 3 * hd :]
        part_out[m, :, 3 * hd :] = squares
        part_copy(m).start()
        return total[:, : 3 * hd], squares

    def combine(m, carry):
        total, squares = carry
        part_copy(m).wait_recv()
        return total + part_in[m, :, : 3 * hd], squares + part_in[m, :, 3 * hd :]

    def ctx_copy(m, i):
        s, t = at_offset(*offsets[i])
        ref = ctx.at[m, :, pl.ds(pl.multiple_of(me * hd, hd), hd)]
        return remote(ref, ref, ctx_send.at[m, i], ctx_recv.at[m, i], {"seq": s, "tp": t})

    query_at = lax.broadcasted_iota(jnp.int32, (toks, toks), 0)
    key_at = lax.broadcasted_iota(jnp.int32, (toks, toks), 1)

    def attend(m, carry):
        total, squares = carry
        bias = jnp.concatenate([q_bias[...], kv_bias[...]], axis=1).astype(jnp.float32)
        cosine = table[0]
        signed_sine = table[1]
        mean = jnp.sum(squares, axis=1, keepdims=True) / (width * members)
        biased = total * lax.rsqrt(mean + EPS) + bias
        queries = rotate(biased[:, :hd], cosine, signed_sine).astype(jnp.bfloat16)
        keys = rotate(biased[:, hd : 2 * hd], cosine, signed_sine).astype(jnp.bfloat16)
        values = biased[:, 2 * hd :].astype(jnp.bfloat16)
        scores = lax.dot_general(
            queries, keys, (((1,), (1,)), ((), ())), preferred_element_type=jnp.float32
        )
        scores = jnp.where(query_at >= key_at, scores * (1.0 / math.sqrt(hd)), -1e30)
        expo = jnp.exp(scores - jnp.max(scores, axis=1, keepdims=True))
        probs = (expo / jnp.sum(expo, axis=1, keepdims=True)).astype(jnp.bfloat16)
        context = jnp.dot(probs, values, preferred_element_type=jnp.float32)
        ctx[m, :, pl.ds(pl.multiple_of(me * hd, hd), hd)] = context.astype(jnp.bfloat16)
        for i in range(len(offsets)):
            ctx_copy(m, i).start()

    def finish(m):
        for i in range(len(offsets)):
            p = source(i)
            ref = ctx.at[m, :, pl.ds(pl.multiple_of(p * hd, hd), hd)]
            remote(ref, ref, ctx_send.at[m, i], ctx_recv.at[m, i], mate).wait_recv()
        for c in range(chunks):
            update = jnp.dot(
                ctx[m], w_out[:, c * cw : (c + 1) * cw], preferred_element_type=jnp.float32
            )
            before = rows[m, own, :, c * cw : (c + 1) * cw].astype(jnp.float32)
            out[0, m * toks : (m + 1) * toks, c * cw : (c + 1) * cw] = (before + update).astype(
                jnp.bfloat16
            )

            @pl.when(sec < sections - 1)
            def _():
                z_copy(m, c).start()

    launch(0)
    for i in range(len(far)):
        k = far_block(i)
        remote(
            gains.at[k], gains.at[k], gain_send.at[i], gain_recv.at[i], mate
        ).wait_recv()

    @pl.when(is_first)
    def _():
        for m in range(1, MICRO):
            embed(m)
            launch(m)

    for load in weights:
        load.wait()
    for copy in weight_copies():
        copy.wait_recv()
    carry = project_first(0)
    for load in loads:
        load.wait()
    for m in range(MICRO):
        carry = project_rest(m, carry)
        if m + 1 < MICRO:

            @pl.when(sec > 0)
            def _():
                launch(m + 1)

        attend(m, combine(m, carry))
        if m + 1 < MICRO:
            carry = project_first(m + 1)
        finish(m)

    for copy in weight_copies():
        copy.wait_send()
    for m in range(MICRO):
        part_copy(m).wait_send()
        for c in range(chunks):
            for i in range(len(far)):
                own_to(m, c, i).wait_send()

            @pl.when(sec < sections - 1)
            def _():
                z_copy(m, c).wait_send()

        for i in range(len(offsets)):
            ctx_copy(m, i).wait_send()
    for i in range(len(far)):
        gain_copy(i).wait_send()

    @pl.when(is_first)
    def _():
        for i in range(len(offsets)):
            for copy in img_copy(i):
                copy.wait_send()


def per_device(
    sizes,
    text_rows,
    image_rows,
    image_target,
    norm_gain,
    q_weight,
    q_bias,
    kv_weight,
    kv_bias,
    out_weight,
):
    sections, seqs, tps = sizes
    members = seqs * tps
    tok_count = text_rows.shape[0] // MICRO
    width = text_rows.shape[1]
    head_size = q_weight.shape[2]
    chunks = 2 if width >= 512 else 1
    features = width * members
    cosine, signed_sine = tables(tok_count, head_size)
    others = members - 1
    half = members // 2
    far = half - 1
    vmem = pl.BlockSpec(memory_space=pltpu.VMEM)
    hbm = pl.BlockSpec(memory_space=pltpu.HBM)
    dma = pltpu.SemaphoreType.DMA
    bf16 = jnp.bfloat16
    return pl.pallas_call(
        functools.partial(kernel, (sections, seqs, tps, chunks)),
        out_shape=jax.ShapeDtypeStruct((1, MICRO * tok_count, width), bf16),
        in_specs=[hbm] * 10,
        out_specs=vmem,
        scratch_shapes=[
            pltpu.VMEM(text_rows.shape, bf16),
            pltpu.SMEM(image_target.shape, jnp.int32),
            pltpu.VMEM(norm_gain.shape, bf16),
            pltpu.VMEM(q_bias.shape, bf16),
            pltpu.VMEM(kv_bias.shape[1:], bf16),
            pltpu.VMEM((2, tok_count, head_size), jnp.float32),
            pltpu.VMEM((half * width, 6 * head_size), bf16),
            pltpu.VMEM((members * head_size, width), bf16),
            pltpu.VMEM((MICRO, half, tok_count, width), bf16),
            pltpu.VMEM((MICRO, tok_count, members * head_size), bf16),
            pltpu.VMEM((MICRO, tok_count, 3 * head_size + LANES), jnp.float32),
            pltpu.VMEM((MICRO, tok_count, 3 * head_size + LANES), jnp.float32),
            pltpu.VMEM((members, image_rows.shape[0], width), bf16),
            pltpu.VMEM((members, 8, LANES), jnp.int32),
            pltpu.VMEM((half, 8, LANES), jnp.float32),
            dma((8 + 2 * half,)),
            dma((MICRO, chunks)),
            dma((MICRO, chunks)),
            dma((MICRO, chunks, far)),
            dma((MICRO, chunks, far)),
            dma((MICRO,)),
            dma((MICRO,)),
            dma((2 * half,)),
            dma((2 * half,)),
            dma((MICRO, others)),
            dma((MICRO, others)),
            dma((far,)),
            dma((far,)),
            dma((others,)),
            dma((members,)),
            dma((others,)),
            dma((others,)),
        ],
        compiler_params=pltpu.CompilerParams(
            collective_id=0, has_side_effects=True, vmem_limit_bytes=60 * 1024 * 1024
        ),
    )(
        text_rows,
        image_rows,
        image_target,
        norm_gain,
        q_weight[0],
        q_bias,
        kv_weight[0].reshape(features, 2 * head_size),
        kv_bias[0],
        out_weight[0],
        jnp.asarray(np.stack([cosine, signed_sine])),
    )


def solution(mesh):
    sizes = tuple(mesh.shape[axis] for axis in ("section", "seq", "tp"))
    in_specs = (
        P(None, ("seq", "tp")),
        P(("seq", "tp"), None),
        P(("seq", "tp")),
        P("section", ("seq", "tp")),
        P("section", None, ("seq", "tp")),
        P("section", ("seq", "tp")),
        P("section", None, "tp", None),
        P("section", "tp", None),
        P("section", None, ("seq", "tp")),
    )
    out_specs = P("section", None, ("seq", "tp"))
    return jax.shard_map(
        functools.partial(per_device, sizes),
        mesh=mesh,
        in_specs=in_specs,
        out_specs=out_specs,
        check_vma=False,
    )
```

```python
import functools
import math

import jax
import jax.numpy as jnp
import numpy as np
from jax import lax
from jax.experimental import pallas as pl
from jax.experimental.pallas import tpu as pltpu
from jax.sharding import PartitionSpec as P

MICRO = 2
EPS = 1e-06
THETA = 1000000.0
LANES = 128
MESH = pl.DeviceIdType.MESH


def tables(tok_count, head_size):
    half_size = head_size // 2
    frequency = np.float32(THETA) ** (
        -np.arange(half_size, dtype=np.float32) * np.float32(2.0) / np.float32(head_size)
    )
    angles = np.arange(tok_count, dtype=np.float32)[:, None] * frequency[None, :]
    cosine = np.concatenate([np.cos(angles), np.cos(angles)], axis=-1)
    signed_sine = np.concatenate([-np.sin(angles), np.sin(angles)], axis=-1)
    return cosine.astype(np.float32), signed_sine.astype(np.float32)


def rotate(values, cosine, signed_sine):
    return values * cosine + pltpu.roll(values, values.shape[1] // 2, 1) * signed_sine


def kernel(
    cfg,
    text_hbm,
    img,
    target_hbm,
    gain_hbm,
    q_hbm,
    q_bias_hbm,
    kv_hbm,
    kv_bias_hbm,
    out_hbm,
    table_hbm,
    out,
    text,
    target,
    gain,
    q_bias,
    kv_bias,
    table,
    w_all,
    w_out,
    rows,
    ctx,
    part_out,
    part_in,
    images,
    marks,
    gains,
    load_sem,
    z_send,
    z_recv,
    far_send,
    far_recv,
    part_send,
    part_recv,
    w_send,
    w_recv,
    ctx_send,
    ctx_recv,
    gain_send,
    gain_recv,
    img_send,
    img_recv,
    mark_send,
    mark_recv,
):
    sections, seqs, tps, chunks = cfg
    members = seqs * tps
    sec = lax.axis_index("section")
    my_s = lax.axis_index("seq")
    my_t = lax.axis_index("tp")
    me = my_s * tps + my_t
    mate = {"seq": my_s, "tp": my_t + 1 - 2 * lax.rem(my_t, 2)}
    mate_t = mate["tp"]
    pairs = tps // 2
    half = seqs * pairs
    own = my_s * pairs + lax.div(my_t, 2)
    toks = text_hbm.shape[0] // MICRO
    width = text_hbm.shape[1]
    cw = width // chunks
    hd = q_hbm.shape[1]
    slots_own = img.shape[0]
    slots = slots_own * members // MICRO
    is_first = sec == 0

    def at_offset(ds, dt, sign=1, base_t=None):
        base = my_t if base_t is None else base_t
        s = lax.rem(my_s + sign * ds + seqs, seqs)
        t = lax.rem(base + sign * dt + tps, tps)
        return s, t

    offsets = [(ds, dt) for ds in range(seqs) for dt in range(tps) if (ds, dt) != (0, 0)]
    far = [(ds, dt) for ds in range(seqs) for dt in range(0, tps, 2) if (ds, dt) != (0, 0)]

    def remote(src, dst, send, recv, device):
        return pltpu.make_async_remote_copy(
            src_ref=src,
            dst_ref=dst,
            send_sem=send,
            recv_sem=recv,
            device_id=device,
            device_id_type=MESH,
        )

    barrier = pltpu.get_barrier_semaphore()
    for ds, dt in offsets:
        s, t = at_offset(ds, dt)
        pl.semaphore_signal(barrier, inc=1, device_id={"seq": s, "tp": t}, device_id_type=MESH)

    @pl.when(sec > 0)
    def _():
        pl.semaphore_signal(barrier, inc=1, device_id={"section": sec - 1}, device_id_type=MESH)

    own_cols = pl.ds(pl.multiple_of(me * width, width), width)
    early = [
        pltpu.make_async_copy(target_hbm, target, load_sem.at[0]),
        pltpu.make_async_copy(gain_hbm, gain, load_sem.at[1]),
        pltpu.make_async_copy(img.at[:, own_cols], images.at[me], load_sem.at[2]),
        pltpu.make_async_copy(text_hbm, text, load_sem.at[3]),
    ]
    loads = [
        pltpu.make_async_copy(q_bias_hbm, q_bias, load_sem.at[4]),
        pltpu.make_async_copy(kv_bias_hbm, kv_bias, load_sem.at[5]),
        pltpu.make_async_copy(table_hbm, table, load_sem.at[6]),
        pltpu.make_async_copy(out_hbm, w_out, load_sem.at[7]),
    ]
    weights = []
    for k in range(half):
        p = lax.div(k, pairs) * tps + lax.rem(k, pairs) * 2 + lax.rem(my_t, 2)
        at = pl.ds(pl.multiple_of(p * width, width), width)
        to = pl.ds(k * width, width)
        weights += [
            pltpu.make_async_copy(q_hbm.at[at, :], w_all.at[to, pl.ds(0, hd)], load_sem.at[8 + 2 * k]),
            pltpu.make_async_copy(
                kv_hbm.at[at, :], w_all.at[to, pl.ds(hd, 2 * hd)], load_sem.at[9 + 2 * k]
            ),
        ]
    for load in early + weights + loads:
        load.start()
    for load in early:
        load.wait()

    for j in range(width // LANES):
        gains[own, j : j + 1, :] = gain[0:1, j * LANES : (j + 1) * LANES].astype(jnp.float32)
    lane = lax.broadcasted_iota(jnp.int32, (8, LANES), 1)
    row = lax.broadcasted_iota(jnp.int32, (8, LANES), 0)
    tile = jnp.full((8, LANES), -1, jnp.int32)
    for k in range(slots_own):
        spot = me * slots_own + k
        here = (row == lax.div(spot, slots)) & (lane == lax.rem(spot, slots))
        tile = jnp.where(here, target[k], tile)
    marks[me] = tile

    @pl.when(sec == sections - 1)
    def _():
        pl.semaphore_wait(barrier, members - 1)

    @pl.when(sec < sections - 1)
    def _():
        pl.semaphore_wait(barrier, members)

    def img_copy(i):
        s, t = at_offset(*offsets[i])
        peer = s * tps + t
        cols = pl.ds(pl.multiple_of(peer * width, width), width)
        dev = {"seq": s, "tp": t}
        return (
            remote(marks.at[me], marks.at[me], mark_send.at[i], mark_recv.at[i], dev),
            remote(img.at[:, cols], images.at[me], img_send.at[i], img_recv.at[me], dev),
        )

    def gain_copy(i):
        s, t = at_offset(*far[i])
        return remote(
            gains.at[own], gains.at[own], gain_send.at[i], gain_recv.at[i], {"seq": s, "tp": t}
        )

    def weight_copies():
        copies = []
        for k in range(half):
            p = lax.div(k, pairs) * tps + lax.rem(k, pairs) * 2 + lax.rem(mate_t, 2)
            at = pl.ds(pl.multiple_of(p * width, width), width)
            to = pl.ds(k * width, width)
            copies += [
                remote(
                    q_hbm.at[at, :],
                    w_all.at[to, pl.ds(3 * hd, hd)],
                    w_send.at[2 * k],
                    w_recv.at[2 * k],
                    mate,
                ),
                remote(
                    kv_hbm.at[at, :],
                    w_all.at[to, pl.ds(4 * hd, 2 * hd)],
                    w_send.at[2 * k + 1],
                    w_recv.at[2 * k + 1],
                    mate,
                ),
            ]
        return copies

    def source(i):
        s, t = at_offset(*offsets[i], sign=-1)
        return s * tps + t

    @pl.when(is_first)
    def _():
        for i in range(len(offsets)):
            for copy in img_copy(i):
                copy.start()

    for i in range(len(far)):
        gain_copy(i).start()
    for copy in weight_copies():
        copy.start()

    per_mb = members // MICRO
    position = lax.broadcasted_iota(jnp.int32, (toks, slots), 0)

    def embed(m):
        merged = marks[0]
        for p in range(1, members):
            merged = jnp.maximum(merged, marks[p])
        match = jnp.where(merged[m : m + 1, :slots] == position, 1.0, 0.0)
        for p in range(m * per_mb, (m + 1) * per_mb):

            @pl.when(me != p)
            def _():
                remote(
                    images.at[p], images.at[p], img_send.at[0], img_recv.at[p], mate
                ).wait_recv()

        stack = jnp.concatenate(
            [images[m * per_mb + p].astype(jnp.float32) for p in range(per_mb)], axis=0
        ).astype(jnp.bfloat16)
        placed = jnp.dot(match.astype(jnp.bfloat16), stack, preferred_element_type=jnp.float32)
        is_image = jnp.max(match, axis=1, keepdims=True) > 0.5
        plain = text[m * toks : (m + 1) * toks, :].astype(jnp.float32)
        rows[m, own] = jnp.where(is_image, placed, plain).astype(jnp.bfloat16)

    @pl.when(is_first)
    def _():
        for i in range(len(offsets)):
            p = source(i)
            remote(
                marks.at[p], marks.at[p], mark_send.at[i], mark_recv.at[i], mate
            ).wait_recv()
        embed(0)

    def cols_of(c):
        return pl.ds(c * cw, cw)

    def z_copy(m, c):
        return remote(
            out.at[0, pl.ds(m * toks, toks), cols_of(c)],
            rows.at[m, own, :, cols_of(c)],
            z_send.at[m, c],
            z_recv.at[m, c],
            {"section": lax.rem(sec + 1, sections)},
        )

    def own_to(m, c, i):
        s, t = at_offset(*far[i])
        ref = rows.at[m, own, :, cols_of(c)]
        return remote(
            ref, ref, far_send.at[m, c, i], far_recv.at[m, c, i], {"seq": s, "tp": t}
        )

    def far_block(i):
        s, t = at_offset(*far[i], sign=-1)
        return s * pairs + lax.div(t, 2)

    def launch(m):
        for c in range(chunks):

            @pl.when(sec > 0)
            def _():
                z_copy(m, c).wait_recv()

            for i in range(len(far)):
                own_to(m, c, i).start()

    def block_step(m, k, c, carry):
        total, squares = carry
        piece = rows[m, k, :, c * cw : (c + 1) * cw].astype(jnp.float32)
        first = c * cw // LANES
        scale = jnp.concatenate(
            [gains[k, pl.ds(first + j, 1), :] for j in range(cw // LANES)], axis=1
        )
        for j in range(cw // LANES):
            part = piece[:, j * LANES : (j + 1) * LANES]
            squares = squares + part * part
        weight = w_all[pl.ds(pl.multiple_of(k * width + c * cw, cw), cw), :]
        total = total + jnp.dot(
            (piece * scale).astype(jnp.bfloat16), weight, preferred_element_type=jnp.float32
        )
        return total, squares

    def part_copy(m):
        return remote(part_out.at[m], part_in.at[m], part_send.at[m], part_recv.at[m], mate)

    def take(m, c, carry):
        for i in range(len(far)):
            k = far_block(i)
            ref = rows.at[m, k, :, cols_of(c)]
            remote(ref, ref, far_send.at[m, c, i], far_recv.at[m, c, i], mate).wait_recv()
            carry = block_step(m, k, c, carry)
        return carry

    def project_first(m):
        carry = (
            jnp.zeros((toks, 6 * hd), jnp.float32),
            jnp.zeros((toks, LANES), jnp.float32),
        )
        for c in range(chunks):
            carry = block_step(m, own, c, carry)
        return take(m, 0, carry)

    def project_rest(m, carry):
        for c in range(1, chunks):
            carry = take(m, c, carry)
        total, squares = carry
        part_out[m, :, : 3 * hd] = total[:, 3 * hd :]
        part_out[m, :, 3 * hd :] = squares
        part_copy(m).start()
        return total[:, : 3 * hd], squares

    def combine(m, carry):
        total, squares = carry
        part_copy(m).wait_recv()
        return total + part_in[m, :, : 3 * hd], squares + part_in[m, :, 3 * hd :]

    def ctx_copy(m, i):
        s, t = at_offset(*offsets[i])
        ref = ctx.at[m, :, pl.ds(pl.multiple_of(me * hd, hd), hd)]
        return remote(ref, ref, ctx_send.at[m, i], ctx_recv.at[m, i], {"seq": s, "tp": t})

    query_at = lax.broadcasted_iota(jnp.int32, (toks, toks), 0)
    key_at = lax.broadcasted_iota(jnp.int32, (toks, toks), 1)

    def attend(m, carry):
        total, squares = carry
        bias = jnp.concatenate([q_bias[...], kv_bias[...]], axis=1).astype(jnp.float32)
        cosine = table[0]
        signed_sine = table[1]
        mean = jnp.sum(squares, axis=1, keepdims=True) / (width * members)
        biased = total * lax.rsqrt(mean + EPS) + bias
        queries = rotate(biased[:, :hd], cosine, signed_sine).astype(jnp.bfloat16)
        keys = rotate(biased[:, hd : 2 * hd], cosine, signed_sine).astype(jnp.bfloat16)
        values = biased[:, 2 * hd :].astype(jnp.bfloat16)
        scores = lax.dot_general(
            queries, keys, (((1,), (1,)), ((), ())), preferred_element_type=jnp.float32
        )
        scores = jnp.where(query_at >= key_at, scores * (1.0 / math.sqrt(hd)), -1e30)
        expo = jnp.exp(scores - jnp.max(scores, axis=1, keepdims=True))
        probs = (expo / jnp.sum(expo, axis=1, keepdims=True)).astype(jnp.bfloat16)
        context = jnp.dot(probs, values, preferred_element_type=jnp.float32)
        ctx[m, :, pl.ds(pl.multiple_of(me * hd, hd), hd)] = context.astype(jnp.bfloat16)
        for i in range(len(offsets)):
            ctx_copy(m, i).start()

    def finish(m):
        for i in range(len(offsets)):
            p = source(i)
            ref = ctx.at[m, :, pl.ds(pl.multiple_of(p * hd, hd), hd)]
            remote(ref, ref, ctx_send.at[m, i], ctx_recv.at[m, i], mate).wait_recv()
        for c in range(chunks):
            update = jnp.dot(
                ctx[m], w_out[:, c * cw : (c + 1) * cw], preferred_element_type=jnp.float32
            )
            before = rows[m, own, :, c * cw : (c + 1) * cw].astype(jnp.float32)
            out[0, m * toks : (m + 1) * toks, c * cw : (c + 1) * cw] = (before + update).astype(
                jnp.bfloat16
            )

            @pl.when(sec < sections - 1)
            def _():
                z_copy(m, c).start()

    launch(0)
    for i in range(len(far)):
        k = far_block(i)
        remote(
            gains.at[k], gains.at[k], gain_send.at[i], gain_recv.at[i], mate
        ).wait_recv()

    @pl.when(is_first)
    def _():
        for m in range(1, MICRO):
            embed(m)
            launch(m)

    for load in weights:
        load.wait()
    for copy in weight_copies():
        copy.wait_recv()
    carry = project_first(0)
    for load in loads:
        load.wait()
    for m in range(MICRO):
        carry = project_rest(m, carry)
        attend(m, combine(m, carry))
        if m + 1 < MICRO:

            @pl.when(sec > 0)
            def _():
                launch(m + 1)

        if m + 1 < MICRO:
            carry = project_first(m + 1)
        finish(m)

    for copy in weight_copies():
        copy.wait_send()
    for m in range(MICRO):
        part_copy(m).wait_send()
        for c in range(chunks):
            for i in range(len(far)):
                own_to(m, c, i).wait_send()

            @pl.when(sec < sections - 1)
            def _():
                z_copy(m, c).wait_send()

        for i in range(len(offsets)):
            ctx_copy(m, i).wait_send()
    for i in range(len(far)):
        gain_copy(i).wait_send()

    @pl.when(is_first)
    def _():
        for i in range(len(offsets)):
            for copy in img_copy(i):
                copy.wait_send()


def per_device(
    sizes,
    text_rows,
    image_rows,
    image_target,
    norm_gain,
    q_weight,
    q_bias,
    kv_weight,
    kv_bias,
    out_weight,
):
    sections, seqs, tps = sizes
    members = seqs * tps
    tok_count = text_rows.shape[0] // MICRO
    width = text_rows.shape[1]
    head_size = q_weight.shape[2]
    chunks = max(1, width // 256)
    features = width * members
    cosine, signed_sine = tables(tok_count, head_size)
    others = members - 1
    half = members // 2
    far = half - 1
    vmem = pl.BlockSpec(memory_space=pltpu.VMEM)
    hbm = pl.BlockSpec(memory_space=pltpu.HBM)
    dma = pltpu.SemaphoreType.DMA
    bf16 = jnp.bfloat16
    return pl.pallas_call(
        functools.partial(kernel, (sections, seqs, tps, chunks)),
        out_shape=jax.ShapeDtypeStruct((1, MICRO * tok_count, width), bf16),
        in_specs=[hbm] * 10,
        out_specs=vmem,
        scratch_shapes=[
            pltpu.VMEM(text_rows.shape, bf16),
            pltpu.SMEM(image_target.shape, jnp.int32),
            pltpu.VMEM(norm_gain.shape, bf16),
            pltpu.VMEM(q_bias.shape, bf16),
            pltpu.VMEM(kv_bias.shape[1:], bf16),
            pltpu.VMEM((2, tok_count, head_size), jnp.float32),
            pltpu.VMEM((half * width, 6 * head_size), bf16),
            pltpu.VMEM((members * head_size, width), bf16),
            pltpu.VMEM((MICRO, half, tok_count, width), bf16),
            pltpu.VMEM((MICRO, tok_count, members * head_size), bf16),
            pltpu.VMEM((MICRO, tok_count, 3 * head_size + LANES), jnp.float32),
            pltpu.VMEM((MICRO, tok_count, 3 * head_size + LANES), jnp.float32),
            pltpu.VMEM((members, image_rows.shape[0], width), bf16),
            pltpu.VMEM((members, 8, LANES), jnp.int32),
            pltpu.VMEM((half, 8, LANES), jnp.float32),
            dma((8 + 2 * half,)),
            dma((MICRO, chunks)),
            dma((MICRO, chunks)),
            dma((MICRO, chunks, far)),
            dma((MICRO, chunks, far)),
            dma((MICRO,)),
            dma((MICRO,)),
            dma((2 * half,)),
            dma((2 * half,)),
            dma((MICRO, others)),
            dma((MICRO, others)),
            dma((far,)),
            dma((far,)),
            dma((others,)),
            dma((members,)),
            dma((others,)),
            dma((others,)),
        ],
        compiler_params=pltpu.CompilerParams(
            collective_id=0, has_side_effects=True, vmem_limit_bytes=60 * 1024 * 1024
        ),
    )(
        text_rows,
        image_rows,
        image_target,
        norm_gain,
        q_weight[0],
        q_bias,
        kv_weight[0].reshape(features, 2 * head_size),
        kv_bias[0],
        out_weight[0],
        jnp.asarray(np.stack([cosine, signed_sine])),
    )


def solution(mesh):
    sizes = tuple(mesh.shape[axis] for axis in ("section", "seq", "tp"))
    in_specs = (
        P(None, ("seq", "tp")),
        P(("seq", "tp"), None),
        P(("seq", "tp")),
        P("section", ("seq", "tp")),
        P("section", None, ("seq", "tp")),
        P("section", ("seq", "tp")),
        P("section", None, "tp", None),
        P("section", "tp", None),
        P("section", None, ("seq", "tp")),
    )
    out_specs = P("section", None, ("seq", "tp"))
    return jax.shard_map(
        functools.partial(per_device, sizes),
        mesh=mesh,
        in_specs=in_specs,
        out_specs=out_specs,
        check_vma=False,
    )
```

```python
import functools
import math

import jax
import jax.numpy as jnp
import numpy as np
from jax import lax
from jax.experimental import pallas as pl
from jax.experimental.pallas import tpu as pltpu
from jax.sharding import PartitionSpec as P

MICRO = 2
EPS = 1e-06
THETA = 1000000.0
LANES = 128
MESH = pl.DeviceIdType.MESH


def tables(tok_count, head_size):
    half_size = head_size // 2
    frequency = np.float32(THETA) ** (
        -np.arange(half_size, dtype=np.float32) * np.float32(2.0) / np.float32(head_size)
    )
    angles = np.arange(tok_count, dtype=np.float32)[:, None] * frequency[None, :]
    cosine = np.concatenate([np.cos(angles), np.cos(angles)], axis=-1)
    signed_sine = np.concatenate([-np.sin(angles), np.sin(angles)], axis=-1)
    return cosine.astype(np.float32), signed_sine.astype(np.float32)


def rotate(values, cosine, signed_sine):
    return values * cosine + pltpu.roll(values, values.shape[1] // 2, 1) * signed_sine


def kernel(
    cfg,
    text_hbm,
    img,
    target_hbm,
    gain_hbm,
    q_hbm,
    q_bias_hbm,
    kv_hbm,
    kv_bias_hbm,
    out_hbm,
    table_hbm,
    out,
    text,
    target,
    gain,
    q_bias,
    kv_bias,
    table,
    w_all,
    w_out,
    rows,
    ctx,
    part_out,
    part_in,
    images,
    marks,
    gains,
    load_sem,
    z_send,
    z_recv,
    far_send,
    far_recv,
    part_send,
    part_recv,
    w_send,
    w_recv,
    ctx_send,
    ctx_recv,
    gain_send,
    gain_recv,
    img_send,
    img_recv,
    mark_send,
    mark_recv,
):
    sections, seqs, tps, chunks = cfg
    members = seqs * tps
    sec = lax.axis_index("section")
    my_s = lax.axis_index("seq")
    my_t = lax.axis_index("tp")
    me = my_s * tps + my_t
    mate = {"seq": my_s, "tp": my_t + 1 - 2 * lax.rem(my_t, 2)}
    mate_t = mate["tp"]
    pairs = tps // 2
    half = seqs * pairs
    own = my_s * pairs + lax.div(my_t, 2)
    toks = text_hbm.shape[0] // MICRO
    width = text_hbm.shape[1]
    cw = width // chunks
    hd = q_hbm.shape[1]
    slots_own = img.shape[0]
    slots = slots_own * members // MICRO
    is_first = sec == 0

    def at_offset(ds, dt, sign=1, base_t=None):
        base = my_t if base_t is None else base_t
        s = lax.rem(my_s + sign * ds + seqs, seqs)
        t = lax.rem(base + sign * dt + tps, tps)
        return s, t

    offsets = [(ds, dt) for ds in range(seqs) for dt in range(tps) if (ds, dt) != (0, 0)]
    far = [(ds, dt) for ds in range(seqs) for dt in range(0, tps, 2) if (ds, dt) != (0, 0)]

    def remote(src, dst, send, recv, device):
        return pltpu.make_async_remote_copy(
            src_ref=src,
            dst_ref=dst,
            send_sem=send,
            recv_sem=recv,
            device_id=device,
            device_id_type=MESH,
        )

    barrier = pltpu.get_barrier_semaphore()
    for ds, dt in offsets:
        s, t = at_offset(ds, dt)
        pl.semaphore_signal(barrier, inc=1, device_id={"seq": s, "tp": t}, device_id_type=MESH)

    @pl.when(sec > 0)
    def _():
        pl.semaphore_signal(barrier, inc=1, device_id={"section": sec - 1}, device_id_type=MESH)

    own_cols = pl.ds(pl.multiple_of(me * width, width), width)
    early = [
        pltpu.make_async_copy(target_hbm, target, load_sem.at[0]),
        pltpu.make_async_copy(gain_hbm, gain, load_sem.at[1]),
        pltpu.make_async_copy(img.at[:, own_cols], images.at[me], load_sem.at[2]),
        pltpu.make_async_copy(text_hbm, text, load_sem.at[3]),
    ]
    loads = [
        pltpu.make_async_copy(q_bias_hbm, q_bias, load_sem.at[4]),
        pltpu.make_async_copy(kv_bias_hbm, kv_bias, load_sem.at[5]),
        pltpu.make_async_copy(table_hbm, table, load_sem.at[6]),
        pltpu.make_async_copy(out_hbm, w_out, load_sem.at[7]),
    ]
    weights = []
    for k in range(half):
        p = lax.div(k, pairs) * tps + lax.rem(k, pairs) * 2 + lax.rem(my_t, 2)
        at = pl.ds(pl.multiple_of(p * width, width), width)
        to = pl.ds(k * width, width)
        weights += [
            pltpu.make_async_copy(q_hbm.at[at, :], w_all.at[to, pl.ds(0, hd)], load_sem.at[8 + 2 * k]),
            pltpu.make_async_copy(
                kv_hbm.at[at, :], w_all.at[to, pl.ds(hd, 2 * hd)], load_sem.at[9 + 2 * k]
            ),
        ]
    for load in early + weights + loads:
        load.start()
    for load in early:
        load.wait()

    for j in range(width // LANES):
        gains[own, j : j + 1, :] = gain[0:1, j * LANES : (j + 1) * LANES].astype(jnp.float32)
    lane = lax.broadcasted_iota(jnp.int32, (8, LANES), 1)
    row = lax.broadcasted_iota(jnp.int32, (8, LANES), 0)
    tile = jnp.full((8, LANES), -1, jnp.int32)
    for k in range(slots_own):
        spot = me * slots_own + k
        here = (row == lax.div(spot, slots)) & (lane == lax.rem(spot, slots))
        tile = jnp.where(here, target[k], tile)
    marks[me] = tile

    @pl.when(sec == sections - 1)
    def _():
        pl.semaphore_wait(barrier, members - 1)

    @pl.when(sec < sections - 1)
    def _():
        pl.semaphore_wait(barrier, members)

    def img_copy(i):
        s, t = at_offset(*offsets[i])
        peer = s * tps + t
        cols = pl.ds(pl.multiple_of(peer * width, width), width)
        dev = {"seq": s, "tp": t}
        return (
            remote(marks.at[me], marks.at[me], mark_send.at[i], mark_recv.at[i], dev),
            remote(img.at[:, cols], images.at[me], img_send.at[i], img_recv.at[me], dev),
        )

    def gain_copy(i):
        s, t = at_offset(*far[i])
        return remote(
            gains.at[own], gains.at[own], gain_send.at[i], gain_recv.at[i], {"seq": s, "tp": t}
        )

    def weight_pair(k):
        p = lax.div(k, pairs) * tps + lax.rem(k, pairs) * 2 + lax.rem(mate_t, 2)
        at = pl.ds(pl.multiple_of(p * width, width), width)
        to = pl.ds(pl.multiple_of(k * width, width), width)
        return (
            remote(
                q_hbm.at[at, :],
                w_all.at[to, pl.ds(3 * hd, hd)],
                w_send.at[2 * k],
                w_recv.at[2 * k],
                mate,
            ),
            remote(
                kv_hbm.at[at, :],
                w_all.at[to, pl.ds(4 * hd, 2 * hd)],
                w_send.at[2 * k + 1],
                w_recv.at[2 * k + 1],
                mate,
            ),
        )

    def weight_wait(k):
        for copy in weight_pair(k):
            copy.wait_recv()

    def source(i):
        s, t = at_offset(*offsets[i], sign=-1)
        return s * tps + t

    @pl.when(is_first)
    def _():
        for i in range(len(offsets)):
            for copy in img_copy(i):
                copy.start()

    for i in range(len(far)):
        gain_copy(i).start()
    for j in range(half):
        for copy in weight_pair(lax.rem(own + j, half)):
            copy.start()

    per_mb = members // MICRO
    position = lax.broadcasted_iota(jnp.int32, (toks, slots), 0)

    def embed(m):
        merged = marks[0]
        for p in range(1, members):
            merged = jnp.maximum(merged, marks[p])
        match = jnp.where(merged[m : m + 1, :slots] == position, 1.0, 0.0)
        for p in range(m * per_mb, (m + 1) * per_mb):

            @pl.when(me != p)
            def _():
                remote(
                    images.at[p], images.at[p], img_send.at[0], img_recv.at[p], mate
                ).wait_recv()

        stack = jnp.concatenate(
            [images[m * per_mb + p].astype(jnp.float32) for p in range(per_mb)], axis=0
        ).astype(jnp.bfloat16)
        placed = jnp.dot(match.astype(jnp.bfloat16), stack, preferred_element_type=jnp.float32)
        is_image = jnp.max(match, axis=1, keepdims=True) > 0.5
        plain = text[m * toks : (m + 1) * toks, :].astype(jnp.float32)
        rows[m, own] = jnp.where(is_image, placed, plain).astype(jnp.bfloat16)

    @pl.when(is_first)
    def _():
        for i in range(len(offsets)):
            p = source(i)
            remote(
                marks.at[p], marks.at[p], mark_send.at[i], mark_recv.at[i], mate
            ).wait_recv()
        embed(0)

    def cols_of(c):
        return pl.ds(c * cw, cw)

    def z_copy(m, c):
        return remote(
            out.at[0, pl.ds(m * toks, toks), cols_of(c)],
            rows.at[m, own, :, cols_of(c)],
            z_send.at[m, c],
            z_recv.at[m, c],
            {"section": lax.rem(sec + 1, sections)},
        )

    def own_to(m, c, i):
        s, t = at_offset(*far[i])
        ref = rows.at[m, own, :, cols_of(c)]
        return remote(
            ref, ref, far_send.at[m, c, i], far_recv.at[m, c, i], {"seq": s, "tp": t}
        )

    def far_block(i):
        s, t = at_offset(*far[i], sign=-1)
        return s * pairs + lax.div(t, 2)

    def launch(m):
        for c in range(chunks):

            @pl.when(sec > 0)
            def _():
                z_copy(m, c).wait_recv()

            for i in range(len(far)):
                own_to(m, c, i).start()

    def block_step(m, k, c, carry):
        total, squares = carry
        piece = rows[m, k, :, c * cw : (c + 1) * cw].astype(jnp.float32)
        first = c * cw // LANES
        scale = jnp.concatenate(
            [gains[k, pl.ds(first + j, 1), :] for j in range(cw // LANES)], axis=1
        )
        for j in range(cw // LANES):
            part = piece[:, j * LANES : (j + 1) * LANES]
            squares = squares + part * part
        weight = w_all[pl.ds(pl.multiple_of(k * width + c * cw, cw), cw), :]
        total = total + jnp.dot(
            (piece * scale).astype(jnp.bfloat16), weight, preferred_element_type=jnp.float32
        )
        return total, squares

    def part_copy(m):
        return remote(part_out.at[m], part_in.at[m], part_send.at[m], part_recv.at[m], mate)

    def take(m, c, carry):
        for i in range(len(far)):
            k = far_block(i)
            ref = rows.at[m, k, :, cols_of(c)]
            remote(ref, ref, far_send.at[m, c, i], far_recv.at[m, c, i], mate).wait_recv()
            if m == 0 and c == 0:
                weight_wait(k)
            carry = block_step(m, k, c, carry)
        return carry

    def project_first(m):
        carry = (
            jnp.zeros((toks, 6 * hd), jnp.float32),
            jnp.zeros((toks, LANES), jnp.float32),
        )
        if m == 0:
            weight_wait(own)
        for c in range(chunks):
            carry = block_step(m, own, c, carry)
        return take(m, 0, carry)

    def project_rest(m, carry):
        for c in range(1, chunks):
            carry = take(m, c, carry)
        total, squares = carry
        part_out[m, :, : 3 * hd] = total[:, 3 * hd :]
        part_out[m, :, 3 * hd :] = squares
        part_copy(m).start()
        return total[:, : 3 * hd], squares

    def combine(m, carry):
        total, squares = carry
        part_copy(m).wait_recv()
        return total + part_in[m, :, : 3 * hd], squares + part_in[m, :, 3 * hd :]

    def ctx_copy(m, i):
        s, t = at_offset(*offsets[i])
        ref = ctx.at[m, :, pl.ds(pl.multiple_of(me * hd, hd), hd)]
        return remote(ref, ref, ctx_send.at[m, i], ctx_recv.at[m, i], {"seq": s, "tp": t})

    query_at = lax.broadcasted_iota(jnp.int32, (toks, toks), 0)
    key_at = lax.broadcasted_iota(jnp.int32, (toks, toks), 1)

    def attend(m, carry):
        total, squares = carry
        bias = jnp.concatenate([q_bias[...], kv_bias[...]], axis=1).astype(jnp.float32)
        cosine = table[0]
        signed_sine = table[1]
        mean = jnp.sum(squares, axis=1, keepdims=True) / (width * members)
        biased = total * lax.rsqrt(mean + EPS) + bias
        queries = rotate(biased[:, :hd], cosine, signed_sine).astype(jnp.bfloat16)
        keys = rotate(biased[:, hd : 2 * hd], cosine, signed_sine).astype(jnp.bfloat16)
        values = biased[:, 2 * hd :].astype(jnp.bfloat16)
        scores = lax.dot_general(
            queries, keys, (((1,), (1,)), ((), ())), preferred_element_type=jnp.float32
        )
        scores = jnp.where(query_at >= key_at, scores * (1.0 / math.sqrt(hd)), -1e30)
        expo = jnp.exp(scores - jnp.max(scores, axis=1, keepdims=True))
        probs = (expo / jnp.sum(expo, axis=1, keepdims=True)).astype(jnp.bfloat16)
        context = jnp.dot(probs, values, preferred_element_type=jnp.float32)
        ctx[m, :, pl.ds(pl.multiple_of(me * hd, hd), hd)] = context.astype(jnp.bfloat16)
        for i in range(len(offsets)):
            ctx_copy(m, i).start()

    def finish(m):
        for i in range(len(offsets)):
            p = source(i)
            ref = ctx.at[m, :, pl.ds(pl.multiple_of(p * hd, hd), hd)]
            remote(ref, ref, ctx_send.at[m, i], ctx_recv.at[m, i], mate).wait_recv()
        for c in range(chunks):
            update = jnp.dot(
                ctx[m], w_out[:, c * cw : (c + 1) * cw], preferred_element_type=jnp.float32
            )
            before = rows[m, own, :, c * cw : (c + 1) * cw].astype(jnp.float32)
            out[0, m * toks : (m + 1) * toks, c * cw : (c + 1) * cw] = (before + update).astype(
                jnp.bfloat16
            )

            @pl.when(sec < sections - 1)
            def _():
                z_copy(m, c).start()

    launch(0)
    for i in range(len(far)):
        k = far_block(i)
        remote(
            gains.at[k], gains.at[k], gain_send.at[i], gain_recv.at[i], mate
        ).wait_recv()

    @pl.when(is_first)
    def _():
        for m in range(1, MICRO):
            embed(m)
            launch(m)

    for load in weights:
        load.wait()
    carry = project_first(0)
    for load in loads:
        load.wait()
    for m in range(MICRO):
        carry = project_rest(m, carry)
        attend(m, combine(m, carry))
        if m + 1 < MICRO:

            @pl.when(sec > 0)
            def _():
                launch(m + 1)

        if m + 1 < MICRO:
            carry = project_first(m + 1)
        finish(m)

    for k in range(half):
        for copy in weight_pair(k):
            copy.wait_send()
    for m in range(MICRO):
        part_copy(m).wait_send()
        for c in range(chunks):
            for i in range(len(far)):
                own_to(m, c, i).wait_send()

            @pl.when(sec < sections - 1)
            def _():
                z_copy(m, c).wait_send()

        for i in range(len(offsets)):
            ctx_copy(m, i).wait_send()
    for i in range(len(far)):
        gain_copy(i).wait_send()

    @pl.when(is_first)
    def _():
        for i in range(len(offsets)):
            for copy in img_copy(i):
                copy.wait_send()


def per_device(
    sizes,
    text_rows,
    image_rows,
    image_target,
    norm_gain,
    q_weight,
    q_bias,
    kv_weight,
    kv_bias,
    out_weight,
):
    sections, seqs, tps = sizes
    members = seqs * tps
    tok_count = text_rows.shape[0] // MICRO
    width = text_rows.shape[1]
    head_size = q_weight.shape[2]
    chunks = max(1, width // 256)
    features = width * members
    cosine, signed_sine = tables(tok_count, head_size)
    others = members - 1
    half = members // 2
    far = half - 1
    vmem = pl.BlockSpec(memory_space=pltpu.VMEM)
    hbm = pl.BlockSpec(memory_space=pltpu.HBM)
    dma = pltpu.SemaphoreType.DMA
    bf16 = jnp.bfloat16
    return pl.pallas_call(
        functools.partial(kernel, (sections, seqs, tps, chunks)),
        out_shape=jax.ShapeDtypeStruct((1, MICRO * tok_count, width), bf16),
        in_specs=[hbm] * 10,
        out_specs=vmem,
        scratch_shapes=[
            pltpu.VMEM(text_rows.shape, bf16),
            pltpu.SMEM(image_target.shape, jnp.int32),
            pltpu.VMEM(norm_gain.shape, bf16),
            pltpu.VMEM(q_bias.shape, bf16),
            pltpu.VMEM(kv_bias.shape[1:], bf16),
            pltpu.VMEM((2, tok_count, head_size), jnp.float32),
            pltpu.VMEM((half * width, 6 * head_size), bf16),
            pltpu.VMEM((members * head_size, width), bf16),
            pltpu.VMEM((MICRO, half, tok_count, width), bf16),
            pltpu.VMEM((MICRO, tok_count, members * head_size), bf16),
            pltpu.VMEM((MICRO, tok_count, 3 * head_size + LANES), jnp.float32),
            pltpu.VMEM((MICRO, tok_count, 3 * head_size + LANES), jnp.float32),
            pltpu.VMEM((members, image_rows.shape[0], width), bf16),
            pltpu.VMEM((members, 8, LANES), jnp.int32),
            pltpu.VMEM((half, 8, LANES), jnp.float32),
            dma((8 + 2 * half,)),
            dma((MICRO, chunks)),
            dma((MICRO, chunks)),
            dma((MICRO, chunks, far)),
            dma((MICRO, chunks, far)),
            dma((MICRO,)),
            dma((MICRO,)),
            dma((2 * half,)),
            dma((2 * half,)),
            dma((MICRO, others)),
            dma((MICRO, others)),
            dma((far,)),
            dma((far,)),
            dma((others,)),
            dma((members,)),
            dma((others,)),
            dma((others,)),
        ],
        compiler_params=pltpu.CompilerParams(
            collective_id=0, has_side_effects=True, vmem_limit_bytes=60 * 1024 * 1024
        ),
    )(
        text_rows,
        image_rows,
        image_target,
        norm_gain,
        q_weight[0],
        q_bias,
        kv_weight[0].reshape(features, 2 * head_size),
        kv_bias[0],
        out_weight[0],
        jnp.asarray(np.stack([cosine, signed_sine])),
    )


def solution(mesh):
    sizes = tuple(mesh.shape[axis] for axis in ("section", "seq", "tp"))
    in_specs = (
        P(None, ("seq", "tp")),
        P(("seq", "tp"), None),
        P(("seq", "tp")),
        P("section", ("seq", "tp")),
        P("section", None, ("seq", "tp")),
        P("section", ("seq", "tp")),
        P("section", None, "tp", None),
        P("section", "tp", None),
        P("section", None, ("seq", "tp")),
    )
    out_specs = P("section", None, ("seq", "tp"))
    return jax.shard_map(
        functools.partial(per_device, sizes),
        mesh=mesh,
        in_specs=in_specs,
        out_specs=out_specs,
        check_vma=False,
    )
```

```python
import functools
import math

import jax
import jax.numpy as jnp
import numpy as np
from jax import lax
from jax.experimental import pallas as pl
from jax.experimental.pallas import tpu as pltpu
from jax.sharding import PartitionSpec as P

MICRO = 2
EPS = 1e-06
THETA = 1000000.0
LANES = 128
MESH = pl.DeviceIdType.MESH


def tables(tok_count, head_size):
    half_size = head_size // 2
    frequency = np.float32(THETA) ** (
        -np.arange(half_size, dtype=np.float32) * np.float32(2.0) / np.float32(head_size)
    )
    angles = np.arange(tok_count, dtype=np.float32)[:, None] * frequency[None, :]
    cosine = np.concatenate([np.cos(angles), np.cos(angles)], axis=-1)
    signed_sine = np.concatenate([-np.sin(angles), np.sin(angles)], axis=-1)
    return cosine.astype(np.float32), signed_sine.astype(np.float32)


def rotate(values, cosine, signed_sine):
    return values * cosine + pltpu.roll(values, values.shape[1] // 2, 1) * signed_sine


def kernel(
    cfg,
    text_hbm,
    img,
    target_hbm,
    gain_hbm,
    q_hbm,
    q_bias_hbm,
    kv_hbm,
    kv_bias_hbm,
    out_hbm,
    table_hbm,
    out,
    text,
    target,
    gain,
    q_bias,
    kv_bias,
    table,
    w_all,
    w_out,
    rows,
    ctx,
    part_out,
    part_in,
    images,
    marks,
    gains,
    load_sem,
    z_send,
    z_recv,
    far_send,
    far_recv,
    part_send,
    part_recv,
    w_send,
    w_recv,
    ctx_send,
    ctx_recv,
    gain_send,
    gain_recv,
    img_send,
    img_recv,
    mark_send,
    mark_recv,
):
    sections, seqs, tps, chunks = cfg
    members = seqs * tps
    sec = lax.axis_index("section")
    my_s = lax.axis_index("seq")
    my_t = lax.axis_index("tp")
    me = my_s * tps + my_t
    mate = {"seq": my_s, "tp": my_t + 1 - 2 * lax.rem(my_t, 2)}
    mate_t = mate["tp"]
    pairs = tps // 2
    half = seqs * pairs
    own = my_s * pairs + lax.div(my_t, 2)
    toks = text_hbm.shape[0] // MICRO
    width = text_hbm.shape[1]
    cw = width // chunks
    hd = q_hbm.shape[1]
    slots_own = img.shape[0]
    slots = slots_own * members // MICRO
    is_first = sec == 0

    def at_offset(ds, dt, sign=1, base_t=None):
        base = my_t if base_t is None else base_t
        s = lax.rem(my_s + sign * ds + seqs, seqs)
        t = lax.rem(base + sign * dt + tps, tps)
        return s, t

    offsets = [(ds, dt) for ds in range(seqs) for dt in range(tps) if (ds, dt) != (0, 0)]
    far = [(ds, dt) for ds in range(seqs) for dt in range(0, tps, 2) if (ds, dt) != (0, 0)]

    def remote(src, dst, send, recv, device):
        return pltpu.make_async_remote_copy(
            src_ref=src,
            dst_ref=dst,
            send_sem=send,
            recv_sem=recv,
            device_id=device,
            device_id_type=MESH,
        )

    barrier = pltpu.get_barrier_semaphore()
    for ds, dt in offsets:
        s, t = at_offset(ds, dt)
        pl.semaphore_signal(barrier, inc=1, device_id={"seq": s, "tp": t}, device_id_type=MESH)

    @pl.when(sec > 0)
    def _():
        pl.semaphore_signal(barrier, inc=1, device_id={"section": sec - 1}, device_id_type=MESH)

    own_cols = pl.ds(pl.multiple_of(me * width, width), width)
    early = [
        pltpu.make_async_copy(target_hbm, target, load_sem.at[0]),
        pltpu.make_async_copy(gain_hbm, gain, load_sem.at[1]),
        pltpu.make_async_copy(img.at[:, own_cols], images.at[me], load_sem.at[2]),
        pltpu.make_async_copy(text_hbm, text, load_sem.at[3]),
    ]
    loads = [
        pltpu.make_async_copy(q_bias_hbm, q_bias, load_sem.at[4]),
        pltpu.make_async_copy(kv_bias_hbm, kv_bias, load_sem.at[5]),
        pltpu.make_async_copy(table_hbm, table, load_sem.at[6]),
        pltpu.make_async_copy(out_hbm, w_out, load_sem.at[7]),
    ]
    weights = []
    for k in range(half):
        p = lax.div(k, pairs) * tps + lax.rem(k, pairs) * 2 + lax.rem(my_t, 2)
        at = pl.ds(pl.multiple_of(p * width, width), width)
        to = pl.ds(k * width, width)
        weights += [
            pltpu.make_async_copy(q_hbm.at[at, :], w_all.at[to, pl.ds(0, hd)], load_sem.at[8 + 2 * k]),
            pltpu.make_async_copy(
                kv_hbm.at[at, :], w_all.at[to, pl.ds(hd, 2 * hd)], load_sem.at[9 + 2 * k]
            ),
        ]
    for load in early + weights + loads:
        load.start()
    for load in early:
        load.wait()

    for j in range(width // LANES):
        gains[own, j : j + 1, :] = gain[0:1, j * LANES : (j + 1) * LANES].astype(jnp.float32)
    lane = lax.broadcasted_iota(jnp.int32, (8, LANES), 1)
    row = lax.broadcasted_iota(jnp.int32, (8, LANES), 0)
    tile = jnp.full((8, LANES), -1, jnp.int32)
    for k in range(slots_own):
        spot = me * slots_own + k
        here = (row == lax.div(spot, slots)) & (lane == lax.rem(spot, slots))
        tile = jnp.where(here, target[k], tile)
    marks[me] = tile

    @pl.when(sec == sections - 1)
    def _():
        pl.semaphore_wait(barrier, members - 1)

    @pl.when(sec < sections - 1)
    def _():
        pl.semaphore_wait(barrier, members)

    def img_copy(i):
        s, t = at_offset(*offsets[i])
        peer = s * tps + t
        cols = pl.ds(pl.multiple_of(peer * width, width), width)
        dev = {"seq": s, "tp": t}
        return (
            remote(marks.at[me], marks.at[me], mark_send.at[i], mark_recv.at[i], dev),
            remote(img.at[:, cols], images.at[me], img_send.at[i], img_recv.at[me], dev),
        )

    def gain_copy(i):
        s, t = at_offset(*far[i])
        return remote(
            gains.at[own], gains.at[own], gain_send.at[i], gain_recv.at[i], {"seq": s, "tp": t}
        )

    def weight_pair(k):
        p = lax.div(k, pairs) * tps + lax.rem(k, pairs) * 2 + lax.rem(mate_t, 2)
        at = pl.ds(pl.multiple_of(p * width, width), width)
        to = pl.ds(pl.multiple_of(k * width, width), width)
        return (
            remote(
                q_hbm.at[at, :],
                w_all.at[to, pl.ds(3 * hd, hd)],
                w_send.at[2 * k],
                w_recv.at[2 * k],
                mate,
            ),
            remote(
                kv_hbm.at[at, :],
                w_all.at[to, pl.ds(4 * hd, 2 * hd)],
                w_send.at[2 * k + 1],
                w_recv.at[2 * k + 1],
                mate,
            ),
        )

    def weight_wait(k):
        for copy in weight_pair(k):
            copy.wait_recv()

    def source(i):
        s, t = at_offset(*offsets[i], sign=-1)
        return s * tps + t

    @pl.when(is_first)
    def _():
        for i in range(len(offsets)):
            for copy in img_copy(i):
                copy.start()

    for i in range(len(far)):
        gain_copy(i).start()
    def send_weights():
        for j in range(half):
            for copy in weight_pair(lax.rem(own + j, half)):
                copy.start()

    @pl.when(sec > 0)
    def _():
        send_weights()

    per_mb = members // MICRO
    position = lax.broadcasted_iota(jnp.int32, (toks, slots), 0)

    def embed(m):
        merged = marks[0]
        for p in range(1, members):
            merged = jnp.maximum(merged, marks[p])
        match = jnp.where(merged[m : m + 1, :slots] == position, 1.0, 0.0)
        for p in range(m * per_mb, (m + 1) * per_mb):

            @pl.when(me != p)
            def _():
                remote(
                    images.at[p], images.at[p], img_send.at[0], img_recv.at[p], mate
                ).wait_recv()

        stack = jnp.concatenate(
            [images[m * per_mb + p].astype(jnp.float32) for p in range(per_mb)], axis=0
        ).astype(jnp.bfloat16)
        placed = jnp.dot(match.astype(jnp.bfloat16), stack, preferred_element_type=jnp.float32)
        is_image = jnp.max(match, axis=1, keepdims=True) > 0.5
        plain = text[m * toks : (m + 1) * toks, :].astype(jnp.float32)
        rows[m, own] = jnp.where(is_image, placed, plain).astype(jnp.bfloat16)

    @pl.when(is_first)
    def _():
        for i in range(len(offsets)):
            p = source(i)
            remote(
                marks.at[p], marks.at[p], mark_send.at[i], mark_recv.at[i], mate
            ).wait_recv()
        embed(0)

    def cols_of(c):
        return pl.ds(c * cw, cw)

    def z_copy(m, c):
        return remote(
            out.at[0, pl.ds(m * toks, toks), cols_of(c)],
            rows.at[m, own, :, cols_of(c)],
            z_send.at[m, c],
            z_recv.at[m, c],
            {"section": lax.rem(sec + 1, sections)},
        )

    def own_to(m, c, i):
        s, t = at_offset(*far[i])
        ref = rows.at[m, own, :, cols_of(c)]
        return remote(
            ref, ref, far_send.at[m, c, i], far_recv.at[m, c, i], {"seq": s, "tp": t}
        )

    def far_block(i):
        s, t = at_offset(*far[i], sign=-1)
        return s * pairs + lax.div(t, 2)

    def launch(m):
        for c in range(chunks):

            @pl.when(sec > 0)
            def _():
                z_copy(m, c).wait_recv()

            for i in range(len(far)):
                own_to(m, c, i).start()

    def block_step(m, k, c, carry):
        total, squares = carry
        piece = rows[m, k, :, c * cw : (c + 1) * cw].astype(jnp.float32)
        first = c * cw // LANES
        scale = jnp.concatenate(
            [gains[k, pl.ds(first + j, 1), :] for j in range(cw // LANES)], axis=1
        )
        for j in range(cw // LANES):
            part = piece[:, j * LANES : (j + 1) * LANES]
            squares = squares + part * part
        weight = w_all[pl.ds(pl.multiple_of(k * width + c * cw, cw), cw), :]
        total = total + jnp.dot(
            (piece * scale).astype(jnp.bfloat16), weight, preferred_element_type=jnp.float32
        )
        return total, squares

    def part_copy(m):
        return remote(part_out.at[m], part_in.at[m], part_send.at[m], part_recv.at[m], mate)

    def take(m, c, carry):
        for i in range(len(far)):
            k = far_block(i)
            ref = rows.at[m, k, :, cols_of(c)]
            remote(ref, ref, far_send.at[m, c, i], far_recv.at[m, c, i], mate).wait_recv()
            if m == 0 and c == 0:
                weight_wait(k)
            carry = block_step(m, k, c, carry)
        return carry

    def project_first(m):
        carry = (
            jnp.zeros((toks, 6 * hd), jnp.float32),
            jnp.zeros((toks, LANES), jnp.float32),
        )
        if m == 0:
            weight_wait(own)
        for c in range(chunks):
            carry = block_step(m, own, c, carry)
        return take(m, 0, carry)

    def project_rest(m, carry):
        for c in range(1, chunks):
            carry = take(m, c, carry)
        total, squares = carry
        part_out[m, :, : 3 * hd] = total[:, 3 * hd :]
        part_out[m, :, 3 * hd :] = squares
        part_copy(m).start()
        return total[:, : 3 * hd], squares

    def combine(m, carry):
        total, squares = carry
        part_copy(m).wait_recv()
        return total + part_in[m, :, : 3 * hd], squares + part_in[m, :, 3 * hd :]

    def ctx_copy(m, i):
        s, t = at_offset(*offsets[i])
        ref = ctx.at[m, :, pl.ds(pl.multiple_of(me * hd, hd), hd)]
        return remote(ref, ref, ctx_send.at[m, i], ctx_recv.at[m, i], {"seq": s, "tp": t})

    query_at = lax.broadcasted_iota(jnp.int32, (toks, toks), 0)
    key_at = lax.broadcasted_iota(jnp.int32, (toks, toks), 1)

    def attend(m, carry):
        total, squares = carry
        bias = jnp.concatenate([q_bias[...], kv_bias[...]], axis=1).astype(jnp.float32)
        cosine = table[0]
        signed_sine = table[1]
        mean = jnp.sum(squares, axis=1, keepdims=True) / (width * members)
        biased = total * lax.rsqrt(mean + EPS) + bias
        queries = rotate(biased[:, :hd], cosine, signed_sine).astype(jnp.bfloat16)
        keys = rotate(biased[:, hd : 2 * hd], cosine, signed_sine).astype(jnp.bfloat16)
        values = biased[:, 2 * hd :].astype(jnp.bfloat16)
        scores = lax.dot_general(
            queries, keys, (((1,), (1,)), ((), ())), preferred_element_type=jnp.float32
        )
        scores = jnp.where(query_at >= key_at, scores * (1.0 / math.sqrt(hd)), -1e30)
        expo = jnp.exp(scores - jnp.max(scores, axis=1, keepdims=True))
        probs = (expo / jnp.sum(expo, axis=1, keepdims=True)).astype(jnp.bfloat16)
        context = jnp.dot(probs, values, preferred_element_type=jnp.float32)
        ctx[m, :, pl.ds(pl.multiple_of(me * hd, hd), hd)] = context.astype(jnp.bfloat16)
        for i in range(len(offsets)):
            ctx_copy(m, i).start()

    def finish(m):
        for i in range(len(offsets)):
            p = source(i)
            ref = ctx.at[m, :, pl.ds(pl.multiple_of(p * hd, hd), hd)]
            remote(ref, ref, ctx_send.at[m, i], ctx_recv.at[m, i], mate).wait_recv()
        for c in range(chunks):
            update = jnp.dot(
                ctx[m], w_out[:, c * cw : (c + 1) * cw], preferred_element_type=jnp.float32
            )
            before = rows[m, own, :, c * cw : (c + 1) * cw].astype(jnp.float32)
            out[0, m * toks : (m + 1) * toks, c * cw : (c + 1) * cw] = (before + update).astype(
                jnp.bfloat16
            )

            @pl.when(sec < sections - 1)
            def _():
                z_copy(m, c).start()

    launch(0)

    @pl.when(is_first)
    def _():
        send_weights()
        for m in range(1, MICRO):
            embed(m)
            launch(m)

    for i in range(len(far)):
        k = far_block(i)
        remote(
            gains.at[k], gains.at[k], gain_send.at[i], gain_recv.at[i], mate
        ).wait_recv()

    for load in weights:
        load.wait()
    carry = project_first(0)
    for load in loads:
        load.wait()
    for m in range(MICRO):
        carry = project_rest(m, carry)
        attend(m, combine(m, carry))
        if m + 1 < MICRO:

            @pl.when(sec > 0)
            def _():
                launch(m + 1)

        if m + 1 < MICRO:
            carry = project_first(m + 1)
        finish(m)

    for k in range(half):
        for copy in weight_pair(k):
            copy.wait_send()
    for m in range(MICRO):
        part_copy(m).wait_send()
        for c in range(chunks):
            for i in range(len(far)):
                own_to(m, c, i).wait_send()

            @pl.when(sec < sections - 1)
            def _():
                z_copy(m, c).wait_send()

        for i in range(len(offsets)):
            ctx_copy(m, i).wait_send()
    for i in range(len(far)):
        gain_copy(i).wait_send()

    @pl.when(is_first)
    def _():
        for i in range(len(offsets)):
            for copy in img_copy(i):
                copy.wait_send()


def per_device(
    sizes,
    text_rows,
    image_rows,
    image_target,
    norm_gain,
    q_weight,
    q_bias,
    kv_weight,
    kv_bias,
    out_weight,
):
    sections, seqs, tps = sizes
    members = seqs * tps
    tok_count = text_rows.shape[0] // MICRO
    width = text_rows.shape[1]
    head_size = q_weight.shape[2]
    chunks = max(1, width // 256)
    features = width * members
    cosine, signed_sine = tables(tok_count, head_size)
    others = members - 1
    half = members // 2
    far = half - 1
    vmem = pl.BlockSpec(memory_space=pltpu.VMEM)
    hbm = pl.BlockSpec(memory_space=pltpu.HBM)
    dma = pltpu.SemaphoreType.DMA
    bf16 = jnp.bfloat16
    return pl.pallas_call(
        functools.partial(kernel, (sections, seqs, tps, chunks)),
        out_shape=jax.ShapeDtypeStruct((1, MICRO * tok_count, width), bf16),
        in_specs=[hbm] * 10,
        out_specs=vmem,
        scratch_shapes=[
            pltpu.VMEM(text_rows.shape, bf16),
            pltpu.SMEM(image_target.shape, jnp.int32),
            pltpu.VMEM(norm_gain.shape, bf16),
            pltpu.VMEM(q_bias.shape, bf16),
            pltpu.VMEM(kv_bias.shape[1:], bf16),
            pltpu.VMEM((2, tok_count, head_size), jnp.float32),
            pltpu.VMEM((half * width, 6 * head_size), bf16),
            pltpu.VMEM((members * head_size, width), bf16),
            pltpu.VMEM((MICRO, half, tok_count, width), bf16),
            pltpu.VMEM((MICRO, tok_count, members * head_size), bf16),
            pltpu.VMEM((MICRO, tok_count, 3 * head_size + LANES), jnp.float32),
            pltpu.VMEM((MICRO, tok_count, 3 * head_size + LANES), jnp.float32),
            pltpu.VMEM((members, image_rows.shape[0], width), bf16),
            pltpu.VMEM((members, 8, LANES), jnp.int32),
            pltpu.VMEM((half, 8, LANES), jnp.float32),
            dma((8 + 2 * half,)),
            dma((MICRO, chunks)),
            dma((MICRO, chunks)),
            dma((MICRO, chunks, far)),
            dma((MICRO, chunks, far)),
            dma((MICRO,)),
            dma((MICRO,)),
            dma((2 * half,)),
            dma((2 * half,)),
            dma((MICRO, others)),
            dma((MICRO, others)),
            dma((far,)),
            dma((far,)),
            dma((others,)),
            dma((members,)),
            dma((others,)),
            dma((others,)),
        ],
        compiler_params=pltpu.CompilerParams(
            collective_id=0, has_side_effects=True, vmem_limit_bytes=60 * 1024 * 1024
        ),
    )(
        text_rows,
        image_rows,
        image_target,
        norm_gain,
        q_weight[0],
        q_bias,
        kv_weight[0].reshape(features, 2 * head_size),
        kv_bias[0],
        out_weight[0],
        jnp.asarray(np.stack([cosine, signed_sine])),
    )


def solution(mesh):
    sizes = tuple(mesh.shape[axis] for axis in ("section", "seq", "tp"))
    in_specs = (
        P(None, ("seq", "tp")),
        P(("seq", "tp"), None),
        P(("seq", "tp")),
        P("section", ("seq", "tp")),
        P("section", None, ("seq", "tp")),
        P("section", ("seq", "tp")),
        P("section", None, "tp", None),
        P("section", "tp", None),
        P("section", None, ("seq", "tp")),
    )
    out_specs = P("section", None, ("seq", "tp"))
    return jax.shard_map(
        functools.partial(per_device, sizes),
        mesh=mesh,
        in_specs=in_specs,
        out_specs=out_specs,
        check_vma=False,
    )
```
